32 devices in a mesh: seq: 8 (over z, y), head: 4 (over x, core).
Axes of the slice: x: 2, y: 2, z: 4, core: 2. Of those that a mesh axis runs over, the one named last changes fastest.
Arguments:
- queries: float32 [768, 1024], P('head', 'seq'), may hold values from -6 to 6
- keys: float32 [768, 1024], P('head', 'seq'), may hold values from -6 to 6
- values: float32 [768, 1024], P('head', 'seq'), may hold values from -6 to 6
- counts: int32 [8], P('seq'), may hold values from 32 to 128
- out_weight: float32 [768, 768], P('head'), may hold values from -0.3125 to 0.3125
- cotangent: float32 [768, 1024], P('head', 'seq'), may hold values from -6 to 6
Outputs:
- output: float32 [768, 1024], P('head', 'seq')
- query_grad: float32 [768, 1024], P('head', 'seq')
- key_grad: float32 [768, 1024], P('head', 'seq')
- value_grad: float32 [768, 1024], P('head', 'seq')
- weight_grad: float32 [768, 768], P('head')
The draws below stay inside these ranges and needn't reach their ends.
All inputs are finite; a program needn't handle non-finite values.
Results may differ from the reference program's by a relative error of at most 0.0014.
Values sent between devices are 32-bit elements; how exact they have to be, the bound alone decides.
A program may use at most 64 MiB of HBM per device.

```python
from functools import partial
import jax
import jax.numpy as jnp
from jax import lax

D = 768
HEADS = 12
HEAD = 64
TOKENS_PER_SHARD = 128
SPACING_LOCAL = 1
SPACING_CENTRAL = 4
SPACING_WIDE = 16
TOKEN_COUNT = 1024
LENGTH_LOCAL = 256
LENGTH_CENTRAL = 1024
N_SEQ = 8


def drawn_pair(key):
    base = jax.random.fold_in(key, 11)
    first, second = jax.random.split(base, 2)
    query_rows = jax.random.truncated_normal(first, -5.5, 5.5, (TOKEN_COUNT, D), jnp.float32)
    key_rows = jax.random.truncated_normal(second, -5.5, 5.5, (TOKEN_COUNT, D), jnp.float32)
    return (query_rows.T, key_rows.T)


def draw_queries(key, part):
    return drawn_pair(key)[0]


def draw_keys(key, part):
    return drawn_pair(key)[1]


def touch_ends(drawn, rng, low, largest):
    shape = drawn.shape
    spot = [jax.random.randint(jax.random.fold_in(rng, axis), (), 0, shape[axis]) for axis in range(len(shape))]
    drawn = drawn.at[tuple(spot)].set(low)
    longest = shape.index(max(shape))
    spot[longest] = (spot[longest] + 1) % shape[longest]
    return drawn.at[tuple(spot)].set(largest)


def with_spikes(entries, own_key, source, target, shards_of, factor):
    owner, partner = [(jnp.arange(entries.shape[axis_at]) // (entries.shape[axis_at] // shards_of)).reshape([-1 if axis == axis_at else 1 for axis in range(entries.ndim)]) for axis_at in (source, target)]
    chosen = jax.random.permutation(own_key, shards_of)[partner]
    strong = (owner == chosen) | (owner == (partner + shards_of // 2) % shards_of)
    return jnp.where(strong, factor * entries, entries)


def steps_of(key, extent, cuts, low, top_value):
    factor_of = 1.0
    for axis_at, parts in cuts:
        steps = jax.random.uniform(jax.random.fold_in(jax.random.fold_in(key, 6), axis_at), (parts,), jnp.float32, low / len(cuts), top_value / len(cuts))
        factor_of = factor_of * jnp.repeat(jnp.exp(steps), extent[axis_at] // parts).reshape((-1,) + (1,) * (len(extent) - 1 - axis_at))
    return factor_of


def normal_values(own_key, dims, spread, reach, cuts=(), kind=jnp.bfloat16):
    entries = spread * jax.random.normal(own_key, dims, jnp.float32)
    if cuts:
        entries = entries * steps_of(own_key, dims, cuts, -0.22, 0.18)
    return jnp.clip(entries, -reach, reach).astype(kind)


def bell_draw_with(stream_key, shape, width, bound, shards, heavy, held_as=jnp.bfloat16):
    values = width * jax.random.normal(stream_key, shape, jnp.float32)
    if shards:
        values = values * steps_of(stream_key, shape, shards, -0.22, 0.18)
    return jnp.clip(with_spikes(values, jax.random.fold_in(stream_key, 3), *heavy), -bound, bound).astype(held_as)


def setup_inputs(seed: int = 0) -> dict:
    arg_keys = jax.random.split(jax.random.key(seed), 7)
    return {
        "queries": draw_queries(jax.random.fold_in(arg_keys[6], 71), 0),
        "keys": draw_keys(jax.random.fold_in(arg_keys[6], 71), 0),
        "values": normal_values(arg_keys[2], (D, TOKEN_COUNT), 1.0, 6.0, ((0, 4), (1, 8)), jnp.float32),
        "counts": touch_ends(jax.random.randint(arg_keys[3], (N_SEQ,), max(TOKENS_PER_SHARD // 4, SPACING_WIDE), TOKENS_PER_SHARD + 1), jax.random.fold_in(arg_keys[3], 1), max(TOKENS_PER_SHARD // 4, SPACING_WIDE), TOKENS_PER_SHARD).astype(jnp.int32),
        "out_weight": bell_draw_with(arg_keys[4], (D, D), D ** -0.5, 0.3125, ((0, 4),), (0, 1, 4, 2.0), jnp.float32),
        "cotangent": normal_values(arg_keys[5], (D, TOKEN_COUNT), 1.0, 6.0, ((0, 4), (1, 8)), jnp.float32),
    }


PRECISE = lax.Precision.HIGHEST
MASKED_SCORE = -1e+30

def single_branch(query_per_head, key_per_head, value_per_head, active_rows, current_head, segment_span, spacing_factor):
    length, head_size = query_per_head.shape
    seg_count = length // segment_span
    per_segment = segment_span // spacing_factor
    offset = current_head % spacing_factor

    def select_rows(block):
        shaped = block.reshape((seg_count, per_segment, spacing_factor) + block.shape[1:])
        return lax.dynamic_index_in_dim(shaped, offset, 2, keepdims=False)
    q_sel = select_rows(query_per_head)
    k_sel = select_rows(key_per_head)
    v_sel = select_rows(value_per_head)
    live_sel = select_rows(active_rows)
    scores = jnp.einsum('sqe,ske->sqk', q_sel, k_sel, precision=PRECISE) * head_size ** (-0.5)
    scores = jnp.where(live_sel[:, None, :] > 0.5, scores, MASKED_SCORE)
    row_max = lax.optimization_barrier(jnp.max(scores, axis=-1))
    weights = jnp.exp(scores - row_max[..., None])
    denominator = lax.optimization_barrier(jnp.sum(weights, axis=-1))
    branch_out = jnp.einsum('sqk,ske->sqe', weights, v_sel, precision=PRECISE) / denominator[..., None]
    log_total = row_max + jnp.log(denominator)
    chosen = jnp.arange(spacing_factor, dtype=jnp.int32) == offset
    spread_out = jnp.where(chosen[None, None, :, None], branch_out[:, :, None, :], 0.0).reshape(length, head_size)
    spread_lse = jnp.where(chosen[None, None, :], log_total[:, :, None], MASKED_SCORE).reshape(length)
    return (spread_out, spread_lse)

def one_head(inputs, active_rows):
    query_per_head, key_per_head, value_per_head, current_head = inputs
    branch_pieces = [single_branch(query_per_head, key_per_head, value_per_head, active_rows, current_head, segment_span, spacing_factor) for segment_span, spacing_factor in ((LENGTH_LOCAL, SPACING_LOCAL), (LENGTH_CENTRAL, SPACING_CENTRAL), (TOKEN_COUNT, SPACING_WIDE))]
    stacked = jnp.stack([item[1] for item in branch_pieces])
    row_peak = lax.optimization_barrier(jnp.max(stacked, axis=0))
    combined_lse = row_peak + jnp.log(lax.optimization_barrier(jnp.sum(jnp.exp(stacked - row_peak[None]), axis=0)))
    combined = jnp.zeros_like(query_per_head)
    for spread_out, spread_lse in branch_pieces:
        combined = combined + jnp.exp(spread_lse - combined_lse)[:, None] * spread_out
    return combined * active_rows[:, None]

def reference(queries, keys, values, counts, out_weight, cotangent):
    positions = jnp.arange(TOKEN_COUNT, dtype=jnp.int32)
    active_rows = (positions % TOKENS_PER_SHARD < jnp.repeat(counts, TOKENS_PER_SHARD)).astype(queries.dtype)
    head_ids = jnp.arange(HEADS, dtype=jnp.int32)

    def by_heads(block):
        return block.reshape(TOKEN_COUNT, HEADS, HEAD).transpose(1, 0, 2)

    def forward(q_all, k_all, v_all, weight):
        head_step = jax.checkpoint(partial(one_head, active_rows=active_rows))
        heads_out = lax.map(head_step, (by_heads(q_all), by_heads(k_all), by_heads(v_all), head_ids))
        attended = heads_out.transpose(1, 0, 2).reshape(TOKEN_COUNT, D)
        return jnp.dot(attended, weight, precision=PRECISE, preferred_element_type=jnp.float32)
    output, pullback = jax.vjp(forward, queries.T, keys.T, values.T, out_weight)
    grads = pullback(cotangent.T)
    return (output.T, grads[0].T, grads[1].T, grads[2].T, grads[3])
```

```python
import functools

import jax
import jax.numpy as jnp
from jax import lax
from jax.experimental import pallas as pl
from jax.experimental.pallas import tpu as pltpu
from jax.sharding import PartitionSpec as P

HEAD = 64
SPACING_LOCAL = 1
SPACING_CENTRAL = 4
SPACING_WIDE = 16
LOG2_LOCAL = 1
LOG2_CENTRAL = 4


PRECISE = lax.Precision.HIGHEST
MASKED_SCORE = -1e30


def from_partner(shard, axis, apart):
    return lax.ppermute(shard, axis, [(i, i ^ 1 << apart) for i in range(lax.axis_size(axis))])


def pick_rows(block, chooser):
    spacing = chooser.shape[1]
    if spacing == 1:
        return block
    shaped = block.reshape(block.shape[:-1] + (block.shape[-1] // spacing, spacing))
    factor = chooser.reshape((chooser.shape[0],) + (1,) * (block.ndim - 1) + (spacing,))
    return jnp.sum(shaped * factor, axis=-1)


def place_rows(piece, chooser, filler):
    spacing = chooser.shape[1]
    if spacing == 1:
        return piece
    chosen = (chooser > 0.5).reshape((chooser.shape[0],) + (1,) * (piece.ndim - 1) + (spacing,))
    spread = jnp.where(chosen, piece[..., None], filler)
    return spread.reshape(piece.shape[:-1] + (piece.shape[-1] * spacing,))


def scores_of(query_rows, key_rows, key_live, score_scale):
    raw = jnp.einsum("heq,hek->hqk", query_rows, key_rows, precision=PRECISE) * score_scale
    return jnp.where(key_live[:, None, :] > 0.5, raw, MASKED_SCORE)


def segment_rows(bundle, extras, levels):
    for bit_index in range(levels):
        other_bundle, other_extras = from_partner((bundle, extras), "seq", bit_index)
        bundle = jnp.concatenate([bundle, other_bundle], axis=3)
        extras = jnp.concatenate([extras, other_extras], axis=3)
    return (bundle, extras)


def return_terms(terms, levels):
    for bit_index in reversed(range(levels)):
        half = terms.shape[3] // 2
        arrived = from_partner(terms[:, :, :, half:], "seq", bit_index)
        terms = terms[:, :, :, :half] + arrived
    return terms


def key_side(key_own, value_own, own_live, far_query, far_grad, far_lse, far_delta, score_scale):
    scores = scores_of(far_query, key_own, own_live, score_scale)
    probabilities = jnp.exp(scores - far_lse[:, :, None])
    value_part = jnp.einsum("hqk,heq->hek", probabilities, far_grad, precision=PRECISE)
    prob_grads = jnp.einsum("heq,hek->hqk", far_grad, value_own, precision=PRECISE)
    score_grads = probabilities * (prob_grads - far_delta[:, :, None])
    key_part = score_scale * jnp.einsum("hqk,heq->hek", score_grads, far_query, precision=PRECISE)
    return (key_part, value_part)


def segment_grads_of(query_rows, grad_rows, probabilities, score_grads, levels, score_scale):
    key_terms = score_scale * jnp.einsum("hqk,heq->hek", score_grads, query_rows, precision=PRECISE)
    value_terms = jnp.einsum("hqk,heq->hek", probabilities, grad_rows, precision=PRECISE)
    owned = return_terms(jnp.stack([key_terms, value_terms]), levels)
    return (owned[0], owned[1])


def on_device(queries, keys, values, counts, out_weight, cotangent):
    columns, row_count = queries.shape
    local_heads = columns // HEAD
    score_scale = HEAD ** (-0.5)
    shard_levels = lax.axis_size("seq").bit_length() - 1
    branches = (
        (SPACING_LOCAL, min(LOG2_LOCAL, shard_levels)),
        (SPACING_CENTRAL, min(LOG2_CENTRAL, shard_levels)),
    )
    global_heads = lax.axis_index("head") * local_heads + jnp.arange(local_heads, dtype=jnp.int32)
    active_rows = (jnp.arange(row_count, dtype=jnp.int32) < counts[0]).astype(jnp.float32)
    live_heads = jnp.broadcast_to(active_rows[None, :], (local_heads, row_count))
    q_all = queries.reshape(local_heads, HEAD, row_count)
    k_all = keys.reshape(local_heads, HEAD, row_count)
    v_all = values.reshape(local_heads, HEAD, row_count)

    def chooser_for(spacing):
        offsets = global_heads % spacing
        return (jnp.arange(spacing, dtype=jnp.int32)[None, :] == offsets[:, None]).astype(
            jnp.float32
        )

    remembered = []
    out_list = []
    lse_list = []
    for spacing_factor, levels in branches:
        chooser = chooser_for(spacing_factor)
        query_rows = pick_rows(q_all, chooser)
        key_own = pick_rows(k_all, chooser)
        value_own = pick_rows(v_all, chooser)
        own_live = pick_rows(live_heads, chooser)
        pairs, extras = segment_rows(
            jnp.stack([key_own, value_own]), own_live[None, :, None, :], levels
        )
        key_rows = pairs[0]
        value_rows = pairs[1]
        key_live = extras[0, :, 0, :]
        scores = scores_of(query_rows, key_rows, key_live, score_scale)
        row_max = jnp.max(scores, axis=-1)
        weights = jnp.exp(scores - row_max[..., None])
        denominator = jnp.sum(weights, axis=-1)
        branch_out = (
            jnp.einsum("hqk,hek->heq", weights, value_rows, precision=PRECISE)
            / denominator[:, None, :]
        )
        log_total = row_max + jnp.log(denominator)
        out_list.append(place_rows(branch_out, chooser, 0.0))
        lse_list.append(place_rows(log_total, chooser, MASKED_SCORE))
        remembered.append(
            (
                chooser,
                levels,
                query_rows,
                key_own,
                value_own,
                own_live,
                key_rows,
                value_rows,
                key_live,
            )
        )
    far_chooser = chooser_for(SPACING_WIDE)
    far_query = pick_rows(q_all, far_chooser)
    far_key = pick_rows(k_all, far_chooser)
    far_value = pick_rows(v_all, far_chooser)
    far_live = pick_rows(live_heads, far_chooser)
    far_pairs = jnp.stack([far_key, far_value])
    far_extras = far_live[None, :, None, :]
    far_rows = far_query.shape[2]
    running_max = jnp.full((local_heads, far_rows), MASKED_SCORE, jnp.float32)
    pairs_piece = lax.all_gather(far_pairs, "seq", axis=3, tiled=True)
    extras_piece = lax.all_gather(far_extras, "seq", axis=3, tiled=True)
    absorb_scores = scores_of(far_query, pairs_piece[0], extras_piece[0, :, 0, :], score_scale)
    newest = jnp.maximum(running_max, jnp.max(absorb_scores, axis=-1))
    weights = jnp.exp(absorb_scores - newest[..., None])
    summed = jnp.sum(weights, axis=-1)
    gathered = jnp.einsum("hqk,hek->heq", weights, pairs_piece[1], precision=PRECISE)
    out_list.append(place_rows(gathered / summed[:, None, :], far_chooser, 0.0))
    lse_list.append(place_rows(newest + jnp.log(summed), far_chooser, MASKED_SCORE))
    stacked = jnp.stack(lse_list)
    row_peak = jnp.max(stacked, axis=0)
    combined_lse = row_peak + jnp.log(jnp.sum(jnp.exp(stacked - row_peak[None]), axis=0))
    combined = jnp.zeros((local_heads, HEAD, row_count), jnp.float32)
    for spread_lse, spread_out in zip(lse_list, out_list):
        combined = combined + jnp.exp(spread_lse - combined_lse)[:, None, :] * spread_out
    attended = (combined * active_rows[None, None, :]).reshape(columns, row_count)
    terms = lax.dot_general(
        out_weight,
        attended,
        (((0,), (0,)), ((), ())),
        precision=PRECISE,
        preferred_element_type=jnp.float32,
    )
    output = lax.psum_scatter(terms, "head", scatter_dimension=0, tiled=True)
    full_grad = lax.all_gather(cotangent, "head", axis=0, tiled=True)
    grad_attended = jnp.dot(
        out_weight, full_grad, precision=PRECISE, preferred_element_type=jnp.float32
    )
    weight_local = lax.dot_general(
        attended,
        full_grad,
        (((1,), (1,)), ((), ())),
        precision=PRECISE,
        preferred_element_type=jnp.float32,
    )
    weight_grad = lax.psum(weight_local, "seq")
    grad_all = grad_attended.reshape(local_heads, HEAD, row_count) * active_rows[None, None, :]
    delta_all = jnp.sum(grad_all * combined, axis=1)
    query_grad = jnp.zeros((local_heads, HEAD, row_count), jnp.float32)
    key_grad = jnp.zeros((local_heads, HEAD, row_count), jnp.float32)
    value_grad = jnp.zeros((local_heads, HEAD, row_count), jnp.float32)
    for (
        chooser,
        levels,
        query_rows,
        key_own,
        value_own,
        own_live,
        key_rows,
        value_rows,
        key_live,
    ) in remembered:
        grad_rows = pick_rows(grad_all, chooser)
        lse_rows = pick_rows(combined_lse, chooser)
        delta_rows = pick_rows(delta_all, chooser)
        scores = scores_of(query_rows, key_rows, key_live, score_scale)
        probabilities = jnp.exp(scores - lse_rows[:, :, None])
        prob_grads = jnp.einsum("heq,hek->hqk", grad_rows, value_rows, precision=PRECISE)
        score_grads = probabilities * (prob_grads - delta_rows[:, :, None])
        query_part = score_scale * jnp.einsum(
            "hqk,hek->heq", score_grads, key_rows, precision=PRECISE
        )
        key_part, value_part = segment_grads_of(
            query_rows, grad_rows, probabilities, score_grads, levels, score_scale
        )
        query_grad = query_grad + place_rows(query_part, chooser, 0.0)
        key_grad = key_grad + place_rows(key_part, chooser, 0.0)
        value_grad = value_grad + place_rows(value_part, chooser, 0.0)
    far_grad = pick_rows(grad_all, far_chooser)
    far_lse = pick_rows(combined_lse, far_chooser)
    far_delta = pick_rows(delta_all, far_chooser)
    pairs_piece = lax.all_gather(far_pairs, "seq", axis=3, tiled=True)
    extras_piece = lax.all_gather(far_extras, "seq", axis=3, tiled=True)
    scores = scores_of(far_query, pairs_piece[0], extras_piece[0, :, 0, :], score_scale)
    probabilities = jnp.exp(scores - far_lse[:, :, None])
    prob_grads = jnp.einsum("heq,hek->hqk", far_grad, pairs_piece[1], precision=PRECISE)
    score_grads = probabilities * (prob_grads - far_delta[:, :, None])
    far_query_part = score_scale * jnp.einsum(
        "hqk,hek->heq", score_grads, pairs_piece[0], precision=PRECISE
    )
    far_bundle = jnp.stack([far_query, far_grad])
    far_stats = jnp.stack([far_lse, far_delta])[:, :, None, :]
    bundle_piece = lax.all_gather(far_bundle, "seq", axis=3, tiled=True)
    stats_piece = lax.all_gather(far_stats, "seq", axis=3, tiled=True)
    key_part, value_part = key_side(
        far_key,
        far_value,
        far_live,
        bundle_piece[0],
        bundle_piece[1],
        stats_piece[0, :, 0, :],
        stats_piece[1, :, 0, :],
        score_scale,
    )
    query_grad = query_grad + place_rows(far_query_part, far_chooser, 0.0)
    key_grad = key_grad + place_rows(key_part, far_chooser, 0.0)
    value_grad = value_grad + place_rows(value_part, far_chooser, 0.0)
    return (
        output,
        query_grad.reshape(columns, row_count),
        key_grad.reshape(columns, row_count),
        value_grad.reshape(columns, row_count),
        weight_grad,
    )


MESH = pl.DeviceIdType.MESH
NN = ((1,), (0,))
TN = ((0,), (0,))
NT = ((1,), (1,))


def product(a, b, dims):
    def once(x, y):
        return lax.dot_general(
            x, y, (dims, ((), ())), preferred_element_type=jnp.float32
        )

    a_top, b_top = a.astype(jnp.bfloat16), b.astype(jnp.bfloat16)
    a_rest = (a - a_top.astype(jnp.float32)).astype(jnp.bfloat16)
    b_rest = (b - b_top.astype(jnp.float32)).astype(jnp.bfloat16)
    return once(a_top, b_top) + (once(a_top, b_rest) + once(a_rest, b_top))


def fused_kernel(
    n_seq, n_head,
    q_hbm, k_hbm, v_hbm, count_ref, w_hbm, cot_hbm,
    out_ref, dq_ref, dk_ref, dv_ref, dw_ref,
    q_ref, k_ref, v_ref, w_ref, cot_ref, load_sem, counted, send_ct, recv_ct, send_y, recv_y, w_half,
    cot_full, near, grads, kvm, qdm, stats, attended, terms, terms_in, local_w, w_in,
    send_cot, recv_cot, send_near, recv_near, send_kv, recv_kv, send_qd, recv_qd,
    send_st, recv_st, send_w, recv_w, send_g, recv_g, send_o, recv_o,
):
    columns, rows = q_ref.shape
    heads = columns // HEAD
    picked = rows // SPACING_CENTRAL
    n_far = n_seq // 2
    loads = [
        pltpu.make_async_copy(src, dst, load_sem.at[i])
        for i, (src, dst) in enumerate(
            ((k_hbm, k_ref), (v_hbm, v_ref), (cot_hbm, cot_ref), (q_hbm, q_ref), (w_hbm, w_ref))
        )
    ]
    for load in loads:
        load.start()
    scale = HEAD ** (-0.5)
    me = lax.axis_index("seq")
    mine = lax.axis_index("head")
    side, height = me % 2, me // 2
    partner = me + 1 - 2 * side

    def at(start, size):
        return pl.ds(pl.multiple_of(start * size, size), size)

    barrier = pltpu.get_barrier_semaphore()
    for k in range(1, n_seq):
        pl.semaphore_signal(
            barrier, inc=1, device_id={"seq": lax.rem(me + k, n_seq)}, device_id_type=MESH
        )
    for k in range(1, n_head):
        pl.semaphore_signal(
            barrier, inc=1, device_id={"head": lax.rem(mine + k, n_head)}, device_id_type=MESH
        )
    offsets = []
    for h in range(heads):
        g = mine * heads + h
        offsets.append((g % SPACING_CENTRAL, g % SPACING_WIDE))
    pick_row = lax.broadcasted_iota(jnp.int32, (picked, rows), 0)
    pick_col = lax.broadcasted_iota(jnp.int32, (picked, rows), 1)
    chooser = [
        jnp.where(pick_col == SPACING_CENTRAL * pick_row + o, 1.0, 0.0) for o, _ in offsets
    ]
    count = jnp.full((picked, rows), count_ref[0], jnp.int32).astype(jnp.float32)
    lane = lax.broadcasted_iota(jnp.int32, (1, rows), 1)
    sub = lax.broadcasted_iota(jnp.int32, (rows, 1), 0).astype(jnp.float32)
    live_row = jnp.where(lane.astype(jnp.float32) < count[0:1, :], 1.0, 0.0)
    live_col = sub < count[0:1, 0:1]

    def hs(h):
        return slice(h * HEAD, (h + 1) * HEAD)

    loads[0].wait()
    loads[1].wait()
    for h in range(heads):
        both = jnp.concatenate([k_ref[hs(h), :], v_ref[hs(h), :]], axis=0)
        kvm[h, at(me, picked), :] = product(chooser[h], both, NT)
    counted[0, at(me, 8), :] = count[0:8, :]
    loads[2].wait()
    loads[3].wait()
    loads[4].wait()
    pl.semaphore_wait(barrier, n_seq + n_head - 2)

    def over_seq(k, src, dst, send, recv):
        return pltpu.make_async_remote_copy(
            src_ref=src, dst_ref=dst, send_sem=send.at[k], recv_sem=recv.at[k],
            device_id={"seq": lax.rem(me + k, n_seq)}, device_id_type=MESH,
        )

    def over_head(k, src, dst, send, recv):
        return pltpu.make_async_remote_copy(
            src_ref=src, dst_ref=dst, send_sem=send.at[k], recv_sem=recv.at[k],
            device_id={"head": lax.rem(mine + k, n_head)}, device_id_type=MESH,
        )

    def to_partner(k, src):
        return pltpu.make_async_remote_copy(
            src_ref=src, dst_ref=near.at[k], send_sem=send_near.at[k],
            recv_sem=recv_near.at[k], device_id={"seq": partner}, device_id_type=MESH,
        )

    def source(k):
        return lax.rem(me + n_seq - k, n_seq)

    def spread(buffer, send, recv, size):
        out = []
        for k in range(1, n_seq):
            block = buffer.at[:, at(me, size), :]
            copy = over_seq(k, block, block, send, recv)
            copy.start()
            out.append(copy)
        return out

    def gathered(buffer, send, recv, size):
        for k in range(1, n_seq):
            block = buffer.at[:, at(source(k), size), :]
            over_seq(k, block, block, send, recv).wait_recv()

    def level(k):
        return 2 * lax.rem(height + k, n_far) + side

    def level_from(k):
        return 2 * lax.rem(height + n_far - k, n_far) + side

    def across(k, block, send, recv):
        return pltpu.make_async_remote_copy(
            src_ref=block, dst_ref=block, send_sem=send.at[k], recv_sem=recv.at[k],
            device_id={"seq": level(k)}, device_id_type=MESH,
        )

    def beside(k, src, dst, send, recv):
        return pltpu.make_async_remote_copy(
            src_ref=src, dst_ref=dst, send_sem=send.at[n_far + k], recv_sem=recv.at[n_far + k],
            device_id={"seq": partner}, device_id_type=MESH,
        )

    def piece(buffer, owner):
        return buffer.at[:, at(owner, picked), :]

    def begin(buffer, send, recv):
        own = piece(buffer, me)
        out = [across(k, own, send, recv) for k in range(1, n_far)]
        out.append(beside(0, own, own, send, recv))
        for copy in out:
            copy.start()
        return out

    def forward(buffer, send, recv):
        out = []
        for k in range(1, n_far):
            block = piece(buffer, level_from(k))
            across(k, block, send, recv).wait_recv()
            copy = beside(k, block, block, send, recv)
            copy.start()
            out.append(copy)
        return out

    def finish(buffer, send, recv):
        for k in range(n_far):
            owner = level_from(k) + 1 - 2 * side
            block = piece(buffer, owner)
            beside(k, block, block, send, recv).wait_recv()

    sent = []
    for k in range(1, n_head):
        copy = over_head(k, cot_ref, cot_full.at[at(mine, columns), :], send_cot, recv_cot)
        copy.start()
        sent.append(copy)
    sent += begin(kvm, send_kv, recv_kv)
    sent += spread(counted, send_ct, recv_ct, 8)
    near_copies = [to_partner(0, k_ref), to_partner(1, v_ref), to_partner(2, q_ref)]
    near_copies[0].start()
    near_copies[1].start()
    cot_full[at(mine, columns), :] = cot_ref[...]
    for k in range(1, n_head):
        origin = lax.rem(mine + n_head - k, n_head)
        over_head(
            k, cot_ref, cot_full.at[at(origin, columns), :], send_cot, recv_cot
        ).wait_recv()
    sent += forward(kvm, send_kv, recv_kv)
    full = cot_full[...]
    grads[...] = product(w_ref[...], full, NN) * live_row
    for h in range(heads):
        both = jnp.concatenate([q_ref[hs(h), :], grads[hs(h), :]], axis=0)
        qdm[h, at(me, picked), :] = product(chooser[h], both, NT)
    sent += begin(qdm, send_qd, recv_qd)
    near_copies[2].start()
    near_grads = to_partner(3, grads)
    near_grads.start()

    finish(kvm, send_kv, recv_kv)
    gathered(counted, send_ct, recv_ct, 8)
    near_copies[0].wait_recv()
    near_copies[1].wait_recv()
    total = n_seq * picked
    slot = lax.broadcasted_iota(jnp.int32, (total, 1), 0) % picked
    counts_mid = jnp.concatenate(
        [jnp.broadcast_to(counted[0, 8 * i:8 * i + 1, 0:1], (picked, 1)) for i in range(n_seq)],
        axis=0,
    )
    partner_count = counted[0, at(partner, 8), :][0:1, 0:1]
    live_near = sub < partner_count

    kept = []
    stat_rows = []
    delta_rows = []
    for h in range(heads):
        o, far = offsets[h]
        place = SPACING_CENTRAL * slot + o
        far_slot = jnp.where(place % SPACING_WIDE == far, 1.0, 0.0)
        live_mid = jnp.where(place.astype(jnp.float32) < counts_mid, 1.0, 0.0)
        in_mid = jnp.where(lane % SPACING_CENTRAL == o, 1.0, 0.0)
        in_far = jnp.where(lane % SPACING_WIDE == far, 1.0, 0.0)
        times = live_mid * (in_mid + far_slot * in_far)
        q = q_ref[hs(h), :]
        d = grads[hs(h), :]
        km = kvm[h, :, 0:HEAD]
        vm = kvm[h, :, HEAD:2 * HEAD]
        k0, v0 = k_ref[hs(h), :], v_ref[hs(h), :]
        k1, v1 = near[0, hs(h), :], near[1, hs(h), :]
        sm = jnp.where(times > 0.5, product(km, q, NN) * scale, MASKED_SCORE)
        s0 = jnp.where(live_col, product(k0, q, TN) * scale, MASKED_SCORE)
        s1 = jnp.where(live_near, product(k1, q, TN) * scale, MASKED_SCORE)
        peak = jnp.maximum(
            jnp.max(sm, axis=0, keepdims=True),
            jnp.maximum(
                jnp.max(s0, axis=0, keepdims=True), jnp.max(s1, axis=0, keepdims=True)
            ),
        )
        wm = times * jnp.exp(sm - peak)
        w0 = jnp.exp(s0 - peak)
        w1 = jnp.exp(s1 - peak)
        bottom = (
            jnp.sum(wm, axis=0, keepdims=True)
            + jnp.sum(w0, axis=0, keepdims=True)
            + jnp.sum(w1, axis=0, keepdims=True)
        )
        inverse = 1.0 / bottom
        pm, p0, p1 = wm * inverse, w0 * inverse, w1 * inverse
        result = product(vm, pm, TN) + product(v0, p0, NN) + product(v1, p1, NN)
        lse = peak + jnp.log(bottom)
        delta = jnp.sum(d * result, axis=0, keepdims=True)
        attended[hs(h), :] = result * live_row
        stat_rows.append(lse)
        delta_rows.append(delta)
        kept.append((km, vm, pm, p0, p1, delta, far_slot, in_mid, in_far))
        if h == 0:
            sent += forward(qdm, send_qd, recv_qd)
    stat_slot = lax.broadcasted_iota(jnp.int32, (8, rows), 0)
    dense = jnp.zeros((8, rows), jnp.float32)
    for i, row in enumerate(stat_rows + delta_rows):
        dense = jnp.where(stat_slot == i, row, dense)
    stats[0, at(me, 8), :] = dense
    chunk = columns // n_seq
    local_w[...] = product(attended[...], full, NT)
    other = 1 - side

    def slab(part, k):
        return at(part * n_far + lax.rem(height + k, n_far), chunk)

    order = list(range(1, n_far)) + [0]
    for k in order:
        copy = beside(k, local_w.at[slab(other, k), :], w_half.at[k], send_y, recv_y)
        copy.start()
        sent.append(copy)
    sent += spread(stats, send_st, recv_st, 8)
    terms[...] = product(w_ref[...], attended[...], TN)
    for k in range(1, n_head):
        copy = over_head(
            k, terms.at[at(lax.rem(mine + k, n_head), columns), :], terms_in.at[k],
            send_o, recv_o,
        )
        copy.start()
        sent.append(copy)

    for k in order:
        beside(k, local_w.at[slab(side, k), :], w_half.at[k], send_y, recv_y).wait_recv()
        w_half[k] = w_half[k] + local_w[slab(side, k), :]
        if k > 0:
            copy = pltpu.make_async_remote_copy(
                src_ref=w_half.at[k], dst_ref=w_in.at[k], send_sem=send_w.at[k],
                recv_sem=recv_w.at[k], device_id={"seq": level(k)}, device_id_type=MESH,
            )
            copy.start()
            sent.append(copy)

    near_copies[2].wait_recv()
    for h in range(heads):
        km, vm, pm, p0, p1, delta, far_slot, in_mid, in_far = kept[h]
        d = grads[hs(h), :]
        q = q_ref[hs(h), :]
        k0, v0 = k_ref[hs(h), :], v_ref[hs(h), :]
        k1, v1 = near[0, hs(h), :], near[1, hs(h), :]
        gm = pm * (product(vm, d, NN) - delta)
        g0 = p0 * (product(v0, d, TN) - delta)
        g1 = p1 * (product(v1, d, TN) - delta)
        dq_ref[hs(h), :] = scale * (
            product(km, gm, TN) + product(k0, g0, NN) + product(k1, g1, NN)
        )
        dk_ref[hs(h), :] = product(q, g0, NT)
        dv_ref[hs(h), :] = product(d, p0, NT)

    summed = w_half[0]
    for k in range(1, n_far):
        pltpu.make_async_remote_copy(
            src_ref=w_half.at[k], dst_ref=w_in.at[k], send_sem=send_w.at[k],
            recv_sem=recv_w.at[k], device_id={"seq": level(k)}, device_id_type=MESH,
        ).wait_recv()
        summed = summed + w_in[k]
    dw_ref[slab(side, 0), :] = summed
    own_slab = dw_ref.at[slab(side, 0), :]
    starts = [across(k, own_slab, send_g, recv_g) for k in range(1, n_far)]
    starts.append(beside(0, own_slab, own_slab, send_g, recv_g))
    for copy in starts:
        copy.start()
    sent += starts

    finish(qdm, send_qd, recv_qd)
    gathered(stats, send_st, recv_st, 8)
    near_grads.wait_recv()
    def relay():
        for k in range(1, n_far):
            block = dw_ref.at[slab(side, n_far - k), :]
            across(k, block, send_g, recv_g).wait_recv()
            copy = beside(k, block, block, send_g, recv_g)
            copy.start()
            sent.append(copy)

    if heads < 2:
        relay()
    theirs = stats[0, at(partner, 8), :]
    for h in range(heads):
        _, _, _, _, _, _, far_slot, in_mid, in_far = kept[h]
        k0, v0 = k_ref[hs(h), :], v_ref[hs(h), :]
        q1, d1 = near[2, hs(h), :], near[3, hs(h), :]
        lse1 = theirs[h:h + 1, :]
        delta1 = theirs[heads + h:heads + h + 1, :]
        sx = jnp.where(live_col, product(k0, q1, TN) * scale, MASKED_SCORE)
        px = jnp.exp(sx - lse1)
        gx = px * (product(v0, d1, TN) - delta1)
        qm = qdm[h, :, 0:HEAD]
        dm = qdm[h, :, HEAD:2 * HEAD]
        times = live_row * (in_mid + far_slot * in_far)
        sy = jnp.where(times > 0.5, product(qm, k0, NN) * scale, MASKED_SCORE)
        lse_col, delta_col = [
            jnp.concatenate(
                [
                    jnp.sum(chooser[h] * stats[0, 8 * i + j:8 * i + j + 1, :], axis=1, keepdims=True)
                    for i in range(n_seq)
                ],
                axis=0,
            )
            for j in (h, heads + h)
        ]
        py = times * jnp.exp(sy - lse_col)
        gy = py * (product(dm, v0, NN) - delta_col)
        dk_ref[hs(h), :] = scale * (
            dk_ref[hs(h), :] + product(q1, gx, NT) + product(qm, gy, TN)
        )
        dv_ref[hs(h), :] = dv_ref[hs(h), :] + product(d1, px, NT) + product(dm, py, TN)
        if h == heads - 2:
            relay()

    output = terms[at(mine, columns), :]
    for k in range(1, n_head):
        over_head(
            k, terms.at[at(mine, columns), :], terms_in.at[k], send_o, recv_o
        ).wait_recv()
    for k in range(1, n_head):
        output = output + terms_in[k]
    out_ref[...] = output
    for k in range(n_far):
        block = dw_ref.at[slab(other, n_far - k), :]
        beside(k, block, block, send_g, recv_g).wait_recv()
    for copy in near_copies + [near_grads] + sent:
        copy.wait_send()


def fused(n_seq, n_head, queries, keys, values, counts, out_weight, cotangent):
    columns, rows = queries.shape
    wide = out_weight.shape[1]
    heads = columns // HEAD
    picked = rows // SPACING_CENTRAL
    chunk = columns // n_seq
    block = jax.ShapeDtypeStruct((columns, rows), jnp.float32)
    vmem = pl.BlockSpec(memory_space=pltpu.VMEM)
    hbm = pl.BlockSpec(memory_space=pltpu.MemorySpace.HBM)
    f32 = jnp.float32
    seq_sem = pltpu.SemaphoreType.DMA((n_seq,))
    head_sem = pltpu.SemaphoreType.DMA((n_head,))
    near_sem = pltpu.SemaphoreType.DMA((4,))
    return pl.pallas_call(
        functools.partial(fused_kernel, n_seq, n_head),
        out_shape=(block, block, block, block, jax.ShapeDtypeStruct((columns, wide), f32)),
        in_specs=[hbm, hbm, hbm, pl.BlockSpec(memory_space=pltpu.SMEM), hbm, hbm],
        out_specs=(vmem,) * 5,
        scratch_shapes=[
            pltpu.VMEM((columns, rows), f32),
            pltpu.VMEM((columns, rows), f32),
            pltpu.VMEM((columns, rows), f32),
            pltpu.VMEM((columns, wide), f32),
            pltpu.VMEM((columns, rows), f32),
            pltpu.SemaphoreType.DMA((5,)),
            pltpu.VMEM((1, n_seq * 8, rows), f32),
            seq_sem, seq_sem, seq_sem, seq_sem,
            pltpu.VMEM((n_seq // 2, chunk, wide), f32),
            pltpu.VMEM((columns * n_head, rows), f32),
            pltpu.VMEM((4, columns, rows), f32),
            pltpu.VMEM((columns, rows), f32),
            pltpu.VMEM((heads, n_seq * picked, rows), f32),
            pltpu.VMEM((heads, n_seq * picked, rows), f32),
            pltpu.VMEM((1, n_seq * 8, rows), f32),
            pltpu.VMEM((columns, rows), f32),
            pltpu.VMEM((wide, rows), f32),
            pltpu.VMEM((n_head, columns, rows), f32),
            pltpu.VMEM((columns, wide), f32),
            pltpu.VMEM((n_seq // 2, chunk, wide), f32),
            head_sem, head_sem, near_sem, near_sem, seq_sem, seq_sem, seq_sem, seq_sem,
            seq_sem, seq_sem, seq_sem, seq_sem, seq_sem, seq_sem, head_sem, head_sem,
        ],
        compiler_params=pltpu.CompilerParams(
            collective_id=0, has_side_effects=True, vmem_limit_bytes=40 * 1024 * 1024
        ),
    )(queries, keys, values, counts, out_weight, cotangent)


def solution(mesh):
    n_seq, n_head = mesh.shape["seq"], mesh.shape["head"]
    whole_is_middle = n_seq <= 1 << LOG2_CENTRAL and n_seq % 2 == 0
    body = functools.partial(fused, n_seq, n_head) if whole_is_middle else on_device
    in_specs = (
        P("head", "seq"),
        P("head", "seq"),
        P("head", "seq"),
        P("seq"),
        P("head", None),
        P("head", "seq"),
    )
    out_specs = (
        P("head", "seq"),
        P("head", "seq"),
        P("head", "seq"),
        P("head", "seq"),
        P("head", None),
    )
    return jax.shard_map(
        body, mesh=mesh, in_specs=in_specs, out_specs=out_specs, check_vma=False
    )
```

```python
import functools

import jax
import jax.numpy as jnp
from jax import lax
from jax.experimental import pallas as pl
from jax.experimental.pallas import tpu as pltpu
from jax.sharding import PartitionSpec as P

HEAD = 64
SPACING_LOCAL = 1
SPACING_CENTRAL = 4
SPACING_WIDE = 16
LOG2_LOCAL = 1
LOG2_CENTRAL = 4


PRECISE = lax.Precision.HIGHEST
MASKED_SCORE = -1e30


def from_partner(shard, axis, apart):
    return lax.ppermute(shard, axis, [(i, i ^ 1 << apart) for i in range(lax.axis_size(axis))])


def pick_rows(block, chooser):
    spacing = chooser.shape[1]
    if spacing == 1:
        return block
    shaped = block.reshape(block.shape[:-1] + (block.shape[-1] // spacing, spacing))
    factor = chooser.reshape((chooser.shape[0],) + (1,) * (block.ndim - 1) + (spacing,))
    return jnp.sum(shaped * factor, axis=-1)


def place_rows(piece, chooser, filler):
    spacing = chooser.shape[1]
    if spacing == 1:
        return piece
    chosen = (chooser > 0.5).reshape((chooser.shape[0],) + (1,) * (piece.ndim - 1) + (spacing,))
    spread = jnp.where(chosen, piece[..., None], filler)
    return spread.reshape(piece.shape[:-1] + (piece.shape[-1] * spacing,))


def scores_of(query_rows, key_rows, key_live, score_scale):
    raw = jnp.einsum("heq,hek->hqk", query_rows, key_rows, precision=PRECISE) * score_scale
    return jnp.where(key_live[:, None, :] > 0.5, raw, MASKED_SCORE)


def segment_rows(bundle, extras, levels):
    for bit_index in range(levels):
        other_bundle, other_extras = from_partner((bundle, extras), "seq", bit_index)
        bundle = jnp.concatenate([bundle, other_bundle], axis=3)
        extras = jnp.concatenate([extras, other_extras], axis=3)
    return (bundle, extras)


def return_terms(terms, levels):
    for bit_index in reversed(range(levels)):
        half = terms.shape[3] // 2
        arrived = from_partner(terms[:, :, :, half:], "seq", bit_index)
        terms = terms[:, :, :, :half] + arrived
    return terms


def key_side(key_own, value_own, own_live, far_query, far_grad, far_lse, far_delta, score_scale):
    scores = scores_of(far_query, key_own, own_live, score_scale)
    probabilities = jnp.exp(scores - far_lse[:, :, None])
    value_part = jnp.einsum("hqk,heq->hek", probabilities, far_grad, precision=PRECISE)
    prob_grads = jnp.einsum("heq,hek->hqk", far_grad, value_own, precision=PRECISE)
    score_grads = probabilities * (prob_grads - far_delta[:, :, None])
    key_part = score_scale * jnp.einsum("hqk,heq->hek", score_grads, far_query, precision=PRECISE)
    return (key_part, value_part)


def segment_grads_of(query_rows, grad_rows, probabilities, score_grads, levels, score_scale):
    key_terms = score_scale * jnp.einsum("hqk,heq->hek", score_grads, query_rows, precision=PRECISE)
    value_terms = jnp.einsum("hqk,heq->hek", probabilities, grad_rows, precision=PRECISE)
    owned = return_terms(jnp.stack([key_terms, value_terms]), levels)
    return (owned[0], owned[1])


def on_device(queries, keys, values, counts, out_weight, cotangent):
    columns, row_count = queries.shape
    local_heads = columns // HEAD
    score_scale = HEAD ** (-0.5)
    shard_levels = lax.axis_size("seq").bit_length() - 1
    branches = (
        (SPACING_LOCAL, min(LOG2_LOCAL, shard_levels)),
        (SPACING_CENTRAL, min(LOG2_CENTRAL, shard_levels)),
    )
    global_heads = lax.axis_index("head") * local_heads + jnp.arange(local_heads, dtype=jnp.int32)
    active_rows = (jnp.arange(row_count, dtype=jnp.int32) < counts[0]).astype(jnp.float32)
    live_heads = jnp.broadcast_to(active_rows[None, :], (local_heads, row_count))
    q_all = queries.reshape(local_heads, HEAD, row_count)
    k_all = keys.reshape(local_heads, HEAD, row_count)
    v_all = values.reshape(local_heads, HEAD, row_count)

    def chooser_for(spacing):
        offsets = global_heads % spacing
        return (jnp.arange(spacing, dtype=jnp.int32)[None, :] == offsets[:, None]).astype(
            jnp.float32
        )

    remembered = []
    out_list = []
    lse_list = []
    for spacing_factor, levels in branches:
        chooser = chooser_for(spacing_factor)
        query_rows = pick_rows(q_all, chooser)
        key_own = pick_rows(k_all, chooser)
        value_own = pick_rows(v_all, chooser)
        own_live = pick_rows(live_heads, chooser)
        pairs, extras = segment_rows(
            jnp.stack([key_own, value_own]), own_live[None, :, None, :], levels
        )
        key_rows = pairs[0]
        value_rows = pairs[1]
        key_live = extras[0, :, 0, :]
        scores = scores_of(query_rows, key_rows, key_live, score_scale)
        row_max = jnp.max(scores, axis=-1)
        weights = jnp.exp(scores - row_max[..., None])
        denominator = jnp.sum(weights, axis=-1)
        branch_out = (
            jnp.einsum("hqk,hek->heq", weights, value_rows, precision=PRECISE)
            / denominator[:, None, :]
        )
        log_total = row_max + jnp.log(denominator)
        out_list.append(place_rows(branch_out, chooser, 0.0))
        lse_list.append(place_rows(log_total, chooser, MASKED_SCORE))
        remembered.append(
            (
                chooser,
                levels,
                query_rows,
                key_own,
                value_own,
                own_live,
                key_rows,
                value_rows,
                key_live,
            )
        )
    far_chooser = chooser_for(SPACING_WIDE)
    far_query = pick_rows(q_all, far_chooser)
    far_key = pick_rows(k_all, far_chooser)
    far_value = pick_rows(v_all, far_chooser)
    far_live = pick_rows(live_heads, far_chooser)
    far_pairs = jnp.stack([far_key, far_value])
    far_extras = far_live[None, :, None, :]
    far_rows = far_query.shape[2]
    running_max = jnp.full((local_heads, far_rows), MASKED_SCORE, jnp.float32)
    pairs_piece = lax.all_gather(far_pairs, "seq", axis=3, tiled=True)
    extras_piece = lax.all_gather(far_extras, "seq", axis=3, tiled=True)
    absorb_scores = scores_of(far_query, pairs_piece[0], extras_piece[0, :, 0, :], score_scale)
    newest = jnp.maximum(running_max, jnp.max(absorb_scores, axis=-1))
    weights = jnp.exp(absorb_scores - newest[..., None])
    summed = jnp.sum(weights, axis=-1)
    gathered = jnp.einsum("hqk,hek->heq", weights, pairs_piece[1], precision=PRECISE)
    out_list.append(place_rows(gathered / summed[:, None, :], far_chooser, 0.0))
    lse_list.append(place_rows(newest + jnp.log(summed), far_chooser, MASKED_SCORE))
    stacked = jnp.stack(lse_list)
    row_peak = jnp.max(stacked, axis=0)
    combined_lse = row_peak + jnp.log(jnp.sum(jnp.exp(stacked - row_peak[None]), axis=0))
    combined = jnp.zeros((local_heads, HEAD, row_count), jnp.float32)
    for spread_lse, spread_out in zip(lse_list, out_list):
        combined = combined + jnp.exp(spread_lse - combined_lse)[:, None, :] * spread_out
    attended = (combined * active_rows[None, None, :]).reshape(columns, row_count)
    terms = lax.dot_general(
        out_weight,
        attended,
        (((0,), (0,)), ((), ())),
        precision=PRECISE,
        preferred_element_type=jnp.float32,
    )
    output = lax.psum_scatter(terms, "head", scatter_dimension=0, tiled=True)
    full_grad = lax.all_gather(cotangent, "head", axis=0, tiled=True)
    grad_attended = jnp.dot(
        out_weight, full_grad, precision=PRECISE, preferred_element_type=jnp.float32
    )
    weight_local = lax.dot_general(
        attended,
        full_grad,
        (((1,), (1,)), ((), ())),
        precision=PRECISE,
        preferred_element_type=jnp.float32,
    )
    weight_grad = lax.psum(weight_local, "seq")
    grad_all = grad_attended.reshape(local_heads, HEAD, row_count) * active_rows[None, None, :]
    delta_all = jnp.sum(grad_all * combined, axis=1)
    query_grad = jnp.zeros((local_heads, HEAD, row_count), jnp.float32)
    key_grad = jnp.zeros((local_heads, HEAD, row_count), jnp.float32)
    value_grad = jnp.zeros((local_heads, HEAD, row_count), jnp.float32)
    for (
        chooser,
        levels,
        query_rows,
        key_own,
        value_own,
        own_live,
        key_rows,
        value_rows,
        key_live,
    ) in remembered:
        grad_rows = pick_rows(grad_all, chooser)
        lse_rows = pick_rows(combined_lse, chooser)
        delta_rows = pick_rows(delta_all, chooser)
        scores = scores_of(query_rows, key_rows, key_live, score_scale)
        probabilities = jnp.exp(scores - lse_rows[:, :, None])
        prob_grads = jnp.einsum("heq,hek->hqk", grad_rows, value_rows, precision=PRECISE)
        score_grads = probabilities * (prob_grads - delta_rows[:, :, None])
        query_part = score_scale * jnp.einsum(
            "hqk,hek->heq", score_grads, key_rows, precision=PRECISE
        )
        key_part, value_part = segment_grads_of(
            query_rows, grad_rows, probabilities, score_grads, levels, score_scale
        )
        query_grad = query_grad + place_rows(query_part, chooser, 0.0)
        key_grad = key_grad + place_rows(key_part, chooser, 0.0)
        value_grad = value_grad + place_rows(value_part, chooser, 0.0)
    far_grad = pick_rows(grad_all, far_chooser)
    far_lse = pick_rows(combined_lse, far_chooser)
    far_delta = pick_rows(delta_all, far_chooser)
    pairs_piece = lax.all_gather(far_pairs, "seq", axis=3, tiled=True)
    extras_piece = lax.all_gather(far_extras, "seq", axis=3, tiled=True)
    scores = scores_of(far_query, pairs_piece[0], extras_piece[0, :, 0, :], score_scale)
    probabilities = jnp.exp(scores - far_lse[:, :, None])
    prob_grads = jnp.einsum("heq,hek->hqk", far_grad, pairs_piece[1], precision=PRECISE)
    score_grads = probabilities * (prob_grads - far_delta[:, :, None])
    far_query_part = score_scale * jnp.einsum(
        "hqk,hek->heq", score_grads, pairs_piece[0], precision=PRECISE
    )
    far_bundle = jnp.stack([far_query, far_grad])
    far_stats = jnp.stack([far_lse, far_delta])[:, :, None, :]
    bundle_piece = lax.all_gather(far_bundle, "seq", axis=3, tiled=True)
    stats_piece = lax.all_gather(far_stats, "seq", axis=3, tiled=True)
    key_part, value_part = key_side(
        far_key,
        far_value,
        far_live,
        bundle_piece[0],
        bundle_piece[1],
        stats_piece[0, :, 0, :],
        stats_piece[1, :, 0, :],
        score_scale,
    )
    query_grad = query_grad + place_rows(far_query_part, far_chooser, 0.0)
    key_grad = key_grad + place_rows(key_part, far_chooser, 0.0)
    value_grad = value_grad + place_rows(value_part, far_chooser, 0.0)
    return (
        output,
        query_grad.reshape(columns, row_count),
        key_grad.reshape(columns, row_count),
        value_grad.reshape(columns, row_count),
        weight_grad,
    )


MESH = pl.DeviceIdType.MESH
NN = ((1,), (0,))
TN = ((0,), (0,))
NT = ((1,), (1,))


def product(a, b, dims):
    def once(x, y):
        return lax.dot_general(
            x, y, (dims, ((), ())), preferred_element_type=jnp.float32
        )

    a_top, b_top = a.astype(jnp.bfloat16), b.astype(jnp.bfloat16)
    a_rest = (a - a_top.astype(jnp.float32)).astype(jnp.bfloat16)
    b_rest = (b - b_top.astype(jnp.float32)).astype(jnp.bfloat16)
    return once(a_top, b_top) + (once(a_top, b_rest) + once(a_rest, b_top))


def fused_kernel(
    n_seq, n_head,
    q_hbm, k_hbm, v_hbm, count_ref, w_hbm, cot_hbm,
    out_ref, dq_ref, dk_ref, dv_ref, dw_ref,
    q_ref, k_ref, v_ref, w_ref, cot_ref, load_sem, counted, send_ct, recv_ct, send_y, recv_y, w_half,
    cot_full, near, grads, kvm, qdm, stats, attended, terms, terms_in, local_w, w_in,
    send_cot, recv_cot, send_near, recv_near, send_kv, recv_kv, send_qd, recv_qd,
    send_st, recv_st, send_w, recv_w, send_g, recv_g, send_o, recv_o,
):
    columns, rows = q_ref.shape
    heads = columns // HEAD
    picked = rows // SPACING_CENTRAL
    n_far = n_seq // 2
    loads = [
        pltpu.make_async_copy(src, dst, load_sem.at[i])
        for i, (src, dst) in enumerate(
            ((k_hbm, k_ref), (v_hbm, v_ref), (cot_hbm, cot_ref), (q_hbm, q_ref), (w_hbm, w_ref))
        )
    ]
    for load in loads:
        load.start()
    scale = HEAD ** (-0.5)
    me = lax.axis_index("seq")
    mine = lax.axis_index("head")
    side, height = me % 2, me // 2
    partner = me + 1 - 2 * side

    def at(start, size):
        return pl.ds(pl.multiple_of(start * size, size), size)

    barrier = pltpu.get_barrier_semaphore()
    for k in range(1, n_seq):
        pl.semaphore_signal(
            barrier, inc=1, device_id={"seq": lax.rem(me + k, n_seq)}, device_id_type=MESH
        )
    for k in range(1, n_head):
        pl.semaphore_signal(
            barrier, inc=1, device_id={"head": lax.rem(mine + k, n_head)}, device_id_type=MESH
        )
    offsets = []
    for h in range(heads):
        g = mine * heads + h
        offsets.append((g % SPACING_CENTRAL, g % SPACING_WIDE))
    pick_row = lax.broadcasted_iota(jnp.int32, (picked, rows), 0)
    pick_col = lax.broadcasted_iota(jnp.int32, (picked, rows), 1)
    chooser = [
        jnp.where(pick_col == SPACING_CENTRAL * pick_row + o, 1.0, 0.0) for o, _ in offsets
    ]
    count = jnp.full((picked, rows), count_ref[0], jnp.int32).astype(jnp.float32)
    lane = lax.broadcasted_iota(jnp.int32, (1, rows), 1)
    sub = lax.broadcasted_iota(jnp.int32, (rows, 1), 0).astype(jnp.float32)
    live_row = jnp.where(lane.astype(jnp.float32) < count[0:1, :], 1.0, 0.0)
    live_col = sub < count[0:1, 0:1]

    def hs(h):
        return slice(h * HEAD, (h + 1) * HEAD)

    loads[0].wait()
    loads[1].wait()
    for h in range(heads):
        both = jnp.concatenate([k_ref[hs(h), :], v_ref[hs(h), :]], axis=0)
        kvm[h, at(me, picked), :] = product(chooser[h], both, NT)
    counted[0, at(me, 8), :] = count[0:8, :]
    loads[2].wait()
    loads[3].wait()
    loads[4].wait()
    pl.semaphore_wait(barrier, n_seq + n_head - 2)

    def over_seq(k, src, dst, send, recv):
        return pltpu.make_async_remote_copy(
            src_ref=src, dst_ref=dst, send_sem=send.at[k], recv_sem=recv.at[k],
            device_id={"seq": lax.rem(me + k, n_seq)}, device_id_type=MESH,
        )

    def over_head(k, src, dst, send, recv):
        return pltpu.make_async_remote_copy(
            src_ref=src, dst_ref=dst, send_sem=send.at[k], recv_sem=recv.at[k],
            device_id={"head": lax.rem(mine + k, n_head)}, device_id_type=MESH,
        )

    def to_partner(k, src):
        return pltpu.make_async_remote_copy(
            src_ref=src, dst_ref=near.at[k], send_sem=send_near.at[k],
            recv_sem=recv_near.at[k], device_id={"seq": partner}, device_id_type=MESH,
        )

    def source(k):
        return lax.rem(me + n_seq - k, n_seq)

    def spread(buffer, send, recv, size):
        out = []
        for k in range(1, n_seq):
            block = buffer.at[:, at(me, size), :]
            copy = over_seq(k, block, block, send, recv)
            copy.start()
            out.append(copy)
        return out

    def gathered(buffer, send, recv, size):
        for k in range(1, n_seq):
            block = buffer.at[:, at(source(k), size), :]
            over_seq(k, block, block, send, recv).wait_recv()

    def level(k):
        return 2 * lax.rem(height + k, n_far) + side

    def level_from(k):
        return 2 * lax.rem(height + n_far - k, n_far) + side

    def across(k, block, send, recv):
        return pltpu.make_async_remote_copy(
            src_ref=block, dst_ref=block, send_sem=send.at[k], recv_sem=recv.at[k],
            device_id={"seq": level(k)}, device_id_type=MESH,
        )

    def beside(k, src, dst, send, recv):
        return pltpu.make_async_remote_copy(
            src_ref=src, dst_ref=dst, send_sem=send.at[n_far + k], recv_sem=recv.at[n_far + k],
            device_id={"seq": partner}, device_id_type=MESH,
        )

    def piece(buffer, owner):
        return buffer.at[:, at(owner, picked), :]

    def begin(buffer, send, recv):
        own = piece(buffer, me)
        out = [across(k, own, send, recv) for k in range(1, n_far)]
        out.append(beside(0, own, own, send, recv))
        for copy in out:
            copy.start()
        return out

    def forward(buffer, send, recv):
        out = []
        for k in range(1, n_far):
            block = piece(buffer, level_from(k))
            across(k, block, send, recv).wait_recv()
            copy = beside(k, block, block, send, recv)
            copy.start()
            out.append(copy)
        return out

    def finish(buffer, send, recv):
        for k in range(n_far):
            owner = level_from(k) + 1 - 2 * side
            block = piece(buffer, owner)
            beside(k, block, block, send, recv).wait_recv()

    sent = []
    for k in range(1, n_head):
        copy = over_head(k, cot_ref, cot_full.at[at(mine, columns), :], send_cot, recv_cot)
        copy.start()
        sent.append(copy)
    sent += begin(kvm, send_kv, recv_kv)
    sent += spread(counted, send_ct, recv_ct, 8)
    near_copies = [to_partner(0, k_ref), to_partner(1, v_ref), to_partner(2, q_ref)]
    near_copies[0].start()
    near_copies[1].start()
    cot_full[at(mine, columns), :] = cot_ref[...]
    for k in range(1, n_head):
        origin = lax.rem(mine + n_head - k, n_head)
        over_head(
            k, cot_ref, cot_full.at[at(origin, columns), :], send_cot, recv_cot
        ).wait_recv()
    sent += forward(kvm, send_kv, recv_kv)
    full = cot_full[...]
    grads[...] = product(w_ref[...], full, NN) * live_row
    for h in range(heads):
        both = jnp.concatenate([q_ref[hs(h), :], grads[hs(h), :]], axis=0)
        qdm[h, at(me, picked), :] = product(chooser[h], both, NT)
    sent += begin(qdm, send_qd, recv_qd)
    near_copies[2].start()
    near_grads = to_partner(3, grads)
    near_grads.start()

    finish(kvm, send_kv, recv_kv)
    gathered(counted, send_ct, recv_ct, 8)
    near_copies[0].wait_recv()
    near_copies[1].wait_recv()
    total = n_seq * picked
    slot = lax.broadcasted_iota(jnp.int32, (total, 1), 0) % picked
    counts_mid = jnp.concatenate(
        [jnp.broadcast_to(counted[0, 8 * i:8 * i + 1, 0:1], (picked, 1)) for i in range(n_seq)],
        axis=0,
    )
    partner_count = counted[0, at(partner, 8), :][0:1, 0:1]
    live_near = sub < partner_count

    kept = []
    stat_rows = []
    delta_rows = []
    for h in range(heads):
        o, far = offsets[h]
        place = SPACING_CENTRAL * slot + o
        far_slot = jnp.where(place % SPACING_WIDE == far, 1.0, 0.0)
        live_mid = jnp.where(place.astype(jnp.float32) < counts_mid, 1.0, 0.0)
        in_mid = jnp.where(lane % SPACING_CENTRAL == o, 1.0, 0.0)
        in_far = jnp.where(lane % SPACING_WIDE == far, 1.0, 0.0)
        times = live_mid * (in_mid + far_slot * in_far)
        q = q_ref[hs(h), :]
        d = grads[hs(h), :]
        km = kvm[h, :, 0:HEAD]
        vm = kvm[h, :, HEAD:2 * HEAD]
        k0, v0 = k_ref[hs(h), :], v_ref[hs(h), :]
        k1, v1 = near[0, hs(h), :], near[1, hs(h), :]
        sm = jnp.where(times > 0.5, product(km, q, NN) * scale, MASKED_SCORE)
        s0 = jnp.where(live_col, product(k0, q, TN) * scale, MASKED_SCORE)
        s1 = jnp.where(live_near, product(k1, q, TN) * scale, MASKED_SCORE)
        peak = jnp.maximum(
            jnp.max(sm, axis=0, keepdims=True),
            jnp.maximum(
                jnp.max(s0, axis=0, keepdims=True), jnp.max(s1, axis=0, keepdims=True)
            ),
        )
        wm = times * jnp.exp(sm - peak)
        w0 = jnp.exp(s0 - peak)
        w1 = jnp.exp(s1 - peak)
        bottom = (
            jnp.sum(wm, axis=0, keepdims=True)
            + jnp.sum(w0, axis=0, keepdims=True)
            + jnp.sum(w1, axis=0, keepdims=True)
        )
        inverse = 1.0 / bottom
        pm, p0, p1 = wm * inverse, w0 * inverse, w1 * inverse
        result = product(vm, pm, TN) + product(v0, p0, NN) + product(v1, p1, NN)
        lse = peak + jnp.log(bottom)
        delta = jnp.sum(d * result, axis=0, keepdims=True)
        attended[hs(h), :] = result * live_row
        stat_rows.append(lse)
        delta_rows.append(delta)
        kept.append((km, vm, pm, p0, p1, delta, far_slot, in_mid, in_far))
        if h == 0:
            sent += forward(qdm, send_qd, recv_qd)
    stat_slot = lax.broadcasted_iota(jnp.int32, (8, rows), 0)
    dense = jnp.zeros((8, rows), jnp.float32)
    for i, row in enumerate(stat_rows + delta_rows):
        dense = jnp.where(stat_slot == i, row, dense)
    stats[0, at(me, 8), :] = dense
    chunk = columns // n_seq
    local_w[...] = product(attended[...], full, NT)
    other = 1 - side

    def slab(part, k):
        return at(part * n_far + lax.rem(height + k, n_far), chunk)

    order = list(range(1, n_far)) + [0]
    for k in order:
        copy = beside(k, local_w.at[slab(other, k), :], w_half.at[k], send_y, recv_y)
        copy.start()
        sent.append(copy)
    sent += spread(stats, send_st, recv_st, 8)
    terms[...] = product(w_ref[...], attended[...], TN)
    for k in range(1, n_head):
        copy = over_head(
            k, terms.at[at(lax.rem(mine + k, n_head), columns), :], terms_in.at[k],
            send_o, recv_o,
        )
        copy.start()
        sent.append(copy)

    for k in order:
        beside(k, local_w.at[slab(side, k), :], w_half.at[k], send_y, recv_y).wait_recv()
        w_half[k] = w_half[k] + local_w[slab(side, k), :]
        if k > 0:
            copy = pltpu.make_async_remote_copy(
                src_ref=w_half.at[k], dst_ref=w_in.at[k], send_sem=send_w.at[k],
                recv_sem=recv_w.at[k], device_id={"seq": level(k)}, device_id_type=MESH,
            )
            copy.start()
            sent.append(copy)

    near_copies[2].wait_recv()
    for h in range(heads):
        km, vm, pm, p0, p1, delta, far_slot, in_mid, in_far = kept[h]
        d = grads[hs(h), :]
        q = q_ref[hs(h), :]
        k0, v0 = k_ref[hs(h), :], v_ref[hs(h), :]
        k1, v1 = near[0, hs(h), :], near[1, hs(h), :]
        gm = pm * (product(vm, d, NN) - delta)
        g0 = p0 * (product(v0, d, TN) - delta)
        g1 = p1 * (product(v1, d, TN) - delta)
        dq_ref[hs(h), :] = scale * (
            product(km, gm, TN) + product(k0, g0, NN) + product(k1, g1, NN)
        )
        dk_ref[hs(h), :] = product(q, g0, NT)
        dv_ref[hs(h), :] = product(d, p0, NT)

    summed = w_half[0]
    for k in range(1, n_far):
        pltpu.make_async_remote_copy(
            src_ref=w_half.at[k], dst_ref=w_in.at[k], send_sem=send_w.at[k],
            recv_sem=recv_w.at[k], device_id={"seq": level(k)}, device_id_type=MESH,
        ).wait_recv()
        summed = summed + w_in[k]
    dw_ref[slab(side, 0), :] = summed
    own_slab = dw_ref.at[slab(side, 0), :]
    starts = [across(k, own_slab, send_g, recv_g) for k in range(1, n_far)]
    starts.append(beside(0, own_slab, own_slab, send_g, recv_g))
    for copy in starts:
        copy.start()
    sent += starts

    finish(qdm, send_qd, recv_qd)
    gathered(stats, send_st, recv_st, 8)
    near_grads.wait_recv()
    def relay():
        for k in range(1, n_far):
            block = dw_ref.at[slab(side, n_far - k), :]
            across(k, block, send_g, recv_g).wait_recv()
            copy = beside(k, block, block, send_g, recv_g)
            copy.start()
            sent.append(copy)

    if heads < 2:
        relay()
    theirs = stats[0, at(partner, 8), :]
    for h in range(heads):
        _, _, _, _, _, _, far_slot, in_mid, in_far = kept[h]
        k0, v0 = k_ref[hs(h), :], v_ref[hs(h), :]
        q1, d1 = near[2, hs(h), :], near[3, hs(h), :]
        lse1 = theirs[h:h + 1, :]
        delta1 = theirs[heads + h:heads + h + 1, :]
        sx = jnp.where(live_col, product(k0, q1, TN) * scale, MASKED_SCORE)
        px = jnp.exp(sx - lse1)
        gx = px * (product(v0, d1, TN) - delta1)
        qm = qdm[h, :, 0:HEAD]
        dm = qdm[h, :, HEAD:2 * HEAD]
        times = live_row * (in_mid + far_slot * in_far)
        sy = jnp.where(times > 0.5, product(qm, k0, NN) * scale, MASKED_SCORE)
        lse_col, delta_col = [
            jnp.concatenate(
                [
                    jnp.sum(chooser[h] * stats[0, 8 * i + j:8 * i + j + 1, :], axis=1, keepdims=True)
                    for i in range(n_seq)
                ],
                axis=0,
            )
            for j in (h, heads + h)
        ]
        py = times * jnp.exp(sy - lse_col)
        gy = py * (product(dm, v0, NN) - delta_col)
        dk_ref[hs(h), :] = scale * (
            dk_ref[hs(h), :] + product(q1, gx, NT) + product(qm, gy, TN)
        )
        dv_ref[hs(h), :] = dv_ref[hs(h), :] + product(d1, px, NT) + product(dm, py, TN)
        if h == heads - 2:
            relay()

    output = terms[at(mine, columns), :]
    for k in range(1, n_head):
        over_head(
            k, terms.at[at(mine, columns), :], terms_in.at[k], send_o, recv_o
        ).wait_recv()
    for k in range(1, n_head):
        output = output + terms_in[k]
    out_ref[...] = output
    for k in range(n_far):
        block = dw_ref.at[slab(other, n_far - k), :]
        beside(k, block, block, send_g, recv_g).wait_recv()
    for copy in near_copies + [near_grads] + sent:
        copy.wait_send()


def fused(n_seq, n_head, queries, keys, values, counts, out_weight, cotangent):
    columns, rows = queries.shape
    wide = out_weight.shape[1]
    heads = columns // HEAD
    picked = rows // SPACING_CENTRAL
    chunk = columns // n_seq
    block = jax.ShapeDtypeStruct((columns, rows), jnp.float32)
    vmem = pl.BlockSpec(memory_space=pltpu.VMEM)
    hbm = pl.BlockSpec(memory_space=pltpu.MemorySpace.HBM)
    f32 = jnp.float32
    seq_sem = pltpu.SemaphoreType.DMA((n_seq,))
    head_sem = pltpu.SemaphoreType.DMA((n_head,))
    near_sem = pltpu.SemaphoreType.DMA((4,))
    return pl.pallas_call(
        functools.partial(fused_kernel, n_seq, n_head),
        out_shape=(block, block, block, block, jax.ShapeDtypeStruct((columns, wide), f32)),
        in_specs=[hbm, hbm, hbm, pl.BlockSpec(memory_space=pltpu.SMEM), hbm, hbm],
        out_specs=(vmem,) * 5,
        scratch_shapes=[
            pltpu.VMEM((columns, rows), f32),
            pltpu.VMEM((columns, rows), f32),
            pltpu.VMEM((columns, rows), f32),
            pltpu.VMEM((columns, wide), f32),
            pltpu.VMEM((columns, rows), f32),
            pltpu.SemaphoreType.DMA((5,)),
            pltpu.VMEM((1, n_seq * 8, rows), f32),
            seq_sem, seq_sem, seq_sem, seq_sem,
            pltpu.VMEM((n_seq // 2, chunk, wide), f32),
            pltpu.VMEM((columns * n_head, rows), f32),
            pltpu.VMEM((4, columns, rows), f32),
            pltpu.VMEM((columns, rows), f32),
            pltpu.VMEM((heads, n_seq * picked, rows), f32),
            pltpu.VMEM((heads, n_seq * picked, rows), f32),
            pltpu.VMEM((1, n_seq * 8, rows), f32),
            pltpu.VMEM((columns, rows), f32),
            pltpu.VMEM((wide, rows), f32),
            pltpu.VMEM((n_head, columns, rows), f32),
            pltpu.VMEM((columns, wide), f32),
            pltpu.VMEM((n_seq // 2, chunk, wide), f32),
            head_sem, head_sem, near_sem, near_sem, seq_sem, seq_sem, seq_sem, seq_sem,
            seq_sem, seq_sem, seq_sem, seq_sem, seq_sem, seq_sem, head_sem, head_sem,
        ],
        compiler_params=pltpu.CompilerParams(
            collective_id=0, has_side_effects=True, vmem_limit_bytes=60 * 1024 * 1024
        ),
    )(queries, keys, values, counts, out_weight, cotangent)


def solution(mesh):
    n_seq, n_head = mesh.shape["seq"], mesh.shape["head"]
    whole_is_middle = n_seq <= 1 << LOG2_CENTRAL and n_seq % 2 == 0
    body = functools.partial(fused, n_seq, n_head) if whole_is_middle else on_device
    in_specs = (
        P("head", "seq"),
        P("head", "seq"),
        P("head", "seq"),
        P("seq"),
        P("head", None),
        P("head", "seq"),
    )
    out_specs = (
        P("head", "seq"),
        P("head", "seq"),
        P("head", "seq"),
        P("head", "seq"),
        P("head", None),
    )
    return jax.shard_map(
        body, mesh=mesh, in_specs=in_specs, out_specs=out_specs, check_vma=False
    )
```

```python
import functools

import jax
import jax.numpy as jnp
from jax import lax
from jax.experimental import pallas as pl
from jax.experimental.pallas import tpu as pltpu
from jax.sharding import PartitionSpec as P

HEAD = 64
SPACING_LOCAL = 1
SPACING_CENTRAL = 4
SPACING_WIDE = 16
LOG2_LOCAL = 1
LOG2_CENTRAL = 4


PRECISE = lax.Precision.HIGHEST
MASKED_SCORE = -1e30


def from_partner(shard, axis, apart):
    return lax.ppermute(shard, axis, [(i, i ^ 1 << apart) for i in range(lax.axis_size(axis))])


def pick_rows(block, chooser):
    spacing = chooser.shape[1]
    if spacing == 1:
        return block
    shaped = block.reshape(block.shape[:-1] + (block.shape[-1] // spacing, spacing))
    factor = chooser.reshape((chooser.shape[0],) + (1,) * (block.ndim - 1) + (spacing,))
    return jnp.sum(shaped * factor, axis=-1)


def place_rows(piece, chooser, filler):
    spacing = chooser.shape[1]
    if spacing == 1:
        return piece
    chosen = (chooser > 0.5).reshape((chooser.shape[0],) + (1,) * (piece.ndim - 1) + (spacing,))
    spread = jnp.where(chosen, piece[..., None], filler)
    return spread.reshape(piece.shape[:-1] + (piece.shape[-1] * spacing,))


def scores_of(query_rows, key_rows, key_live, score_scale):
    raw = jnp.einsum("heq,hek->hqk", query_rows, key_rows, precision=PRECISE) * score_scale
    return jnp.where(key_live[:, None, :] > 0.5, raw, MASKED_SCORE)


def segment_rows(bundle, extras, levels):
    for bit_index in range(levels):
        other_bundle, other_extras = from_partner((bundle, extras), "seq", bit_index)
        bundle = jnp.concatenate([bundle, other_bundle], axis=3)
        extras = jnp.concatenate([extras, other_extras], axis=3)
    return (bundle, extras)


def return_terms(terms, levels):
    for bit_index in reversed(range(levels)):
        half = terms.shape[3] // 2
        arrived = from_partner(terms[:, :, :, half:], "seq", bit_index)
        terms = terms[:, :, :, :half] + arrived
    return terms


def key_side(key_own, value_own, own_live, far_query, far_grad, far_lse, far_delta, score_scale):
    scores = scores_of(far_query, key_own, own_live, score_scale)
    probabilities = jnp.exp(scores - far_lse[:, :, None])
    value_part = jnp.einsum("hqk,heq->hek", probabilities, far_grad, precision=PRECISE)
    prob_grads = jnp.einsum("heq,hek->hqk", far_grad, value_own, precision=PRECISE)
    score_grads = probabilities * (prob_grads - far_delta[:, :, None])
    key_part = score_scale * jnp.einsum("hqk,heq->hek", score_grads, far_query, precision=PRECISE)
    return (key_part, value_part)


def segment_grads_of(query_rows, grad_rows, probabilities, score_grads, levels, score_scale):
    key_terms = score_scale * jnp.einsum("hqk,heq->hek", score_grads, query_rows, precision=PRECISE)
    value_terms = jnp.einsum("hqk,heq->hek", probabilities, grad_rows, precision=PRECISE)
    owned = return_terms(jnp.stack([key_terms, value_terms]), levels)
    return (owned[0], owned[1])


def on_device(queries, keys, values, counts, out_weight, cotangent):
    columns, row_count = queries.shape
    local_heads = columns // HEAD
    score_scale = HEAD ** (-0.5)
    shard_levels = lax.axis_size("seq").bit_length() - 1
    branches = (
        (SPACING_LOCAL, min(LOG2_LOCAL, shard_levels)),
        (SPACING_CENTRAL, min(LOG2_CENTRAL, shard_levels)),
    )
    global_heads = lax.axis_index("head") * local_heads + jnp.arange(local_heads, dtype=jnp.int32)
    active_rows = (jnp.arange(row_count, dtype=jnp.int32) < counts[0]).astype(jnp.float32)
    live_heads = jnp.broadcast_to(active_rows[None, :], (local_heads, row_count))
    q_all = queries.reshape(local_heads, HEAD, row_count)
    k_all = keys.reshape(local_heads, HEAD, row_count)
    v_all = values.reshape(local_heads, HEAD, row_count)

    def chooser_for(spacing):
        offsets = global_heads % spacing
        return (jnp.arange(spacing, dtype=jnp.int32)[None, :] == offsets[:, None]).astype(
            jnp.float32
        )

    remembered = []
    out_list = []
    lse_list = []
    for spacing_factor, levels in branches:
        chooser = chooser_for(spacing_factor)
        query_rows = pick_rows(q_all, chooser)
        key_own = pick_rows(k_all, chooser)
        value_own = pick_rows(v_all, chooser)
        own_live = pick_rows(live_heads, chooser)
        pairs, extras = segment_rows(
            jnp.stack([key_own, value_own]), own_live[None, :, None, :], levels
        )
        key_rows = pairs[0]
        value_rows = pairs[1]
        key_live = extras[0, :, 0, :]
        scores = scores_of(query_rows, key_rows, key_live, score_scale)
        row_max = jnp.max(scores, axis=-1)
        weights = jnp.exp(scores - row_max[..., None])
        denominator = jnp.sum(weights, axis=-1)
        branch_out = (
            jnp.einsum("hqk,hek->heq", weights, value_rows, precision=PRECISE)
            / denominator[:, None, :]
        )
        log_total = row_max + jnp.log(denominator)
        out_list.append(place_rows(branch_out, chooser, 0.0))
        lse_list.append(place_rows(log_total, chooser, MASKED_SCORE))
        remembered.append(
            (
                chooser,
                levels,
                query_rows,
                key_own,
                value_own,
                own_live,
                key_rows,
                value_rows,
                key_live,
            )
        )
    far_chooser = chooser_for(SPACING_WIDE)
    far_query = pick_rows(q_all, far_chooser)
    far_key = pick_rows(k_all, far_chooser)
    far_value = pick_rows(v_all, far_chooser)
    far_live = pick_rows(live_heads, far_chooser)
    far_pairs = jnp.stack([far_key, far_value])
    far_extras = far_live[None, :, None, :]
    far_rows = far_query.shape[2]
    running_max = jnp.full((local_heads, far_rows), MASKED_SCORE, jnp.float32)
    pairs_piece = lax.all_gather(far_pairs, "seq", axis=3, tiled=True)
    extras_piece = lax.all_gather(far_extras, "seq", axis=3, tiled=True)
    absorb_scores = scores_of(far_query, pairs_piece[0], extras_piece[0, :, 0, :], score_scale)
    newest = jnp.maximum(running_max, jnp.max(absorb_scores, axis=-1))
    weights = jnp.exp(absorb_scores - newest[..., None])
    summed = jnp.sum(weights, axis=-1)
    gathered = jnp.einsum("hqk,hek->heq", weights, pairs_piece[1], precision=PRECISE)
    out_list.append(place_rows(gathered / summed[:, None, :], far_chooser, 0.0))
    lse_list.append(place_rows(newest + jnp.log(summed), far_chooser, MASKED_SCORE))
    stacked = jnp.stack(lse_list)
    row_peak = jnp.max(stacked, axis=0)
    combined_lse = row_peak + jnp.log(jnp.sum(jnp.exp(stacked - row_peak[None]), axis=0))
    combined = jnp.zeros((local_heads, HEAD, row_count), jnp.float32)
    for spread_lse, spread_out in zip(lse_list, out_list):
        combined = combined + jnp.exp(spread_lse - combined_lse)[:, None, :] * spread_out
    attended = (combined * active_rows[None, None, :]).reshape(columns, row_count)
    terms = lax.dot_general(
        out_weight,
        attended,
        (((0,), (0,)), ((), ())),
        precision=PRECISE,
        preferred_element_type=jnp.float32,
    )
    output = lax.psum_scatter(terms, "head", scatter_dimension=0, tiled=True)
    full_grad = lax.all_gather(cotangent, "head", axis=0, tiled=True)
    grad_attended = jnp.dot(
        out_weight, full_grad, precision=PRECISE, preferred_element_type=jnp.float32
    )
    weight_local = lax.dot_general(
        attended,
        full_grad,
        (((1,), (1,)), ((), ())),
        precision=PRECISE,
        preferred_element_type=jnp.float32,
    )
    weight_grad = lax.psum(weight_local, "seq")
    grad_all = grad_attended.reshape(local_heads, HEAD, row_count) * active_rows[None, None, :]
    delta_all = jnp.sum(grad_all * combined, axis=1)
    query_grad = jnp.zeros((local_heads, HEAD, row_count), jnp.float32)
    key_grad = jnp.zeros((local_heads, HEAD, row_count), jnp.float32)
    value_grad = jnp.zeros((local_heads, HEAD, row_count), jnp.float32)
    for (
        chooser,
        levels,
        query_rows,
        key_own,
        value_own,
        own_live,
        key_rows,
        value_rows,
        key_live,
    ) in remembered:
        grad_rows = pick_rows(grad_all, chooser)
        lse_rows = pick_rows(combined_lse, chooser)
        delta_rows = pick_rows(delta_all, chooser)
        scores = scores_of(query_rows, key_rows, key_live, score_scale)
        probabilities = jnp.exp(scores - lse_rows[:, :, None])
        prob_grads = jnp.einsum("heq,hek->hqk", grad_rows, value_rows, precision=PRECISE)
        score_grads = probabilities * (prob_grads - delta_rows[:, :, None])
        query_part = score_scale * jnp.einsum(
            "hqk,hek->heq", score_grads, key_rows, precision=PRECISE
        )
        key_part, value_part = segment_grads_of(
            query_rows, grad_rows, probabilities, score_grads, levels, score_scale
        )
        query_grad = query_grad + place_rows(query_part, chooser, 0.0)
        key_grad = key_grad + place_rows(key_part, chooser, 0.0)
        value_grad = value_grad + place_rows(value_part, chooser, 0.0)
    far_grad = pick_rows(grad_all, far_chooser)
    far_lse = pick_rows(combined_lse, far_chooser)
    far_delta = pick_rows(delta_all, far_chooser)
    pairs_piece = lax.all_gather(far_pairs, "seq", axis=3, tiled=True)
    extras_piece = lax.all_gather(far_extras, "seq", axis=3, tiled=True)
    scores = scores_of(far_query, pairs_piece[0], extras_piece[0, :, 0, :], score_scale)
    probabilities = jnp.exp(scores - far_lse[:, :, None])
    prob_grads = jnp.einsum("heq,hek->hqk", far_grad, pairs_piece[1], precision=PRECISE)
    score_grads = probabilities * (prob_grads - far_delta[:, :, None])
    far_query_part = score_scale * jnp.einsum(
        "hqk,hek->heq", score_grads, pairs_piece[0], precision=PRECISE
    )
    far_bundle = jnp.stack([far_query, far_grad])
    far_stats = jnp.stack([far_lse, far_delta])[:, :, None, :]
    bundle_piece = lax.all_gather(far_bundle, "seq", axis=3, tiled=True)
    stats_piece = lax.all_gather(far_stats, "seq", axis=3, tiled=True)
    key_part, value_part = key_side(
        far_key,
        far_value,
        far_live,
        bundle_piece[0],
        bundle_piece[1],
        stats_piece[0, :, 0, :],
        stats_piece[1, :, 0, :],
        score_scale,
    )
    query_grad = query_grad + place_rows(far_query_part, far_chooser, 0.0)
    key_grad = key_grad + place_rows(key_part, far_chooser, 0.0)
    value_grad = value_grad + place_rows(value_part, far_chooser, 0.0)
    return (
        output,
        query_grad.reshape(columns, row_count),
        key_grad.reshape(columns, row_count),
        value_grad.reshape(columns, row_count),
        weight_grad,
    )


MESH = pl.DeviceIdType.MESH
NN = ((1,), (0,))
TN = ((0,), (0,))
NT = ((1,), (1,))


def product(a, b, dims):
    def once(x, y):
        return lax.dot_general(
            x, y, (dims, ((), ())), preferred_element_type=jnp.float32
        )

    a_top, b_top = a.astype(jnp.bfloat16), b.astype(jnp.bfloat16)
    a_rest = (a - a_top.astype(jnp.float32)).astype(jnp.bfloat16)
    b_rest = (b - b_top.astype(jnp.float32)).astype(jnp.bfloat16)
    return once(a_top, b_top) + (once(a_top, b_rest) + once(a_rest, b_top))


def fused_kernel(
    n_seq, n_head,
    q_hbm, k_hbm, v_hbm, count_ref, w_hbm, cot_hbm,
    out_ref, dq_ref, dk_ref, dv_ref, dw_ref,
    q_ref, k_ref, v_ref, w_ref, cot_ref, load_sem, counted, send_ct, recv_ct, send_y, recv_y, w_half,
    cot_full, near, grads, kvm, qdm, stats, attended, terms, terms_in, local_w, w_in,
    send_cot, recv_cot, send_near, recv_near, send_kv, recv_kv, send_qd, recv_qd,
    send_st, recv_st, send_w, recv_w, send_g, recv_g, send_o, recv_o,
):
    columns, rows = q_ref.shape
    heads = columns // HEAD
    picked = rows // SPACING_CENTRAL
    n_far = n_seq // 2
    loads = [
        pltpu.make_async_copy(src, dst, load_sem.at[i])
        for i, (src, dst) in enumerate(
            ((k_hbm, k_ref), (v_hbm, v_ref), (cot_hbm, cot_ref), (q_hbm, q_ref), (w_hbm, w_ref))
        )
    ]
    for load in loads:
        load.start()
    scale = HEAD ** (-0.5)
    me = lax.axis_index("seq")
    mine = lax.axis_index("head")
    side, height = me % 2, me // 2
    partner = me + 1 - 2 * side

    def at(start, size):
        return pl.ds(pl.multiple_of(start * size, size), size)

    barrier = pltpu.get_barrier_semaphore()
    for k in range(1, n_seq):
        pl.semaphore_signal(
            barrier, inc=1, device_id={"seq": lax.rem(me + k, n_seq)}, device_id_type=MESH
        )
    for k in range(1, n_head):
        pl.semaphore_signal(
            barrier, inc=1, device_id={"head": lax.rem(mine + k, n_head)}, device_id_type=MESH
        )
    offsets = []
    for h in range(heads):
        g = mine * heads + h
        offsets.append((g % SPACING_CENTRAL, g % SPACING_WIDE))
    pick_row = lax.broadcasted_iota(jnp.int32, (picked, rows), 0)
    pick_col = lax.broadcasted_iota(jnp.int32, (picked, rows), 1)
    chooser = [
        jnp.where(pick_col == SPACING_CENTRAL * pick_row + o, 1.0, 0.0) for o, _ in offsets
    ]
    count = jnp.full((picked, rows), count_ref[0], jnp.int32).astype(jnp.float32)
    lane = lax.broadcasted_iota(jnp.int32, (1, rows), 1)
    sub = lax.broadcasted_iota(jnp.int32, (rows, 1), 0).astype(jnp.float32)
    live_row = jnp.where(lane.astype(jnp.float32) < count[0:1, :], 1.0, 0.0)
    live_col = sub < count[0:1, 0:1]

    def hs(h):
        return slice(h * HEAD, (h + 1) * HEAD)

    loads[0].wait()
    loads[1].wait()
    for h in range(heads):
        both = jnp.concatenate([k_ref[hs(h), :], v_ref[hs(h), :]], axis=0)
        kvm[h, at(me, picked), :] = product(chooser[h], both, NT)
    counted[0, at(me, 8), :] = count[0:8, :]
    loads[2].wait()
    loads[3].wait()
    loads[4].wait()
    pl.semaphore_wait(barrier, n_seq + n_head - 2)

    def over_seq(k, src, dst, send, recv):
        return pltpu.make_async_remote_copy(
            src_ref=src, dst_ref=dst, send_sem=send.at[k], recv_sem=recv.at[k],
            device_id={"seq": lax.rem(me + k, n_seq)}, device_id_type=MESH,
        )

    def over_head(k, src, dst, send, recv):
        return pltpu.make_async_remote_copy(
            src_ref=src, dst_ref=dst, send_sem=send.at[k], recv_sem=recv.at[k],
            device_id={"head": lax.rem(mine + k, n_head)}, device_id_type=MESH,
        )

    def to_partner(k, src):
        return pltpu.make_async_remote_copy(
            src_ref=src, dst_ref=near.at[k], send_sem=send_near.at[k],
            recv_sem=recv_near.at[k], device_id={"seq": partner}, device_id_type=MESH,
        )

    def source(k):
        return lax.rem(me + n_seq - k, n_seq)

    def spread(buffer, send, recv, size):
        out = []
        for k in range(1, n_seq):
            block = buffer.at[:, at(me, size), :]
            copy = over_seq(k, block, block, send, recv)
            copy.start()
            out.append(copy)
        return out

    def gathered(buffer, send, recv, size):
        for k in range(1, n_seq):
            block = buffer.at[:, at(source(k), size), :]
            over_seq(k, block, block, send, recv).wait_recv()

    def level(k):
        return 2 * lax.rem(height + k, n_far) + side

    def level_from(k):
        return 2 * lax.rem(height + n_far - k, n_far) + side

    def across(k, block, send, recv):
        return pltpu.make_async_remote_copy(
            src_ref=block, dst_ref=block, send_sem=send.at[k], recv_sem=recv.at[k],
            device_id={"seq": level(k)}, device_id_type=MESH,
        )

    def beside(k, src, dst, send, recv):
        return pltpu.make_async_remote_copy(
            src_ref=src, dst_ref=dst, send_sem=send.at[n_far + k], recv_sem=recv.at[n_far + k],
            device_id={"seq": partner}, device_id_type=MESH,
        )

    def piece(buffer, owner):
        return buffer.at[:, at(owner, picked), :]

    def begin(buffer, send, recv):
        own = piece(buffer, me)
        out = [across(k, own, send, recv) for k in range(1, n_far)]
        out.append(beside(0, own, own, send, recv))
        for copy in out:
            copy.start()
        return out

    def forward(buffer, send, recv):
        out = []
        for k in range(1, n_far):
            block = piece(buffer, level_from(k))
            across(k, block, send, recv).wait_recv()
            copy = beside(k, block, block, send, recv)
            copy.start()
            out.append(copy)
        return out

    def finish(buffer, send, recv):
        for k in range(n_far):
            owner = level_from(k) + 1 - 2 * side
            block = piece(buffer, owner)
            beside(k, block, block, send, recv).wait_recv()

    sent = []
    for k in range(1, n_head):
        copy = over_head(k, cot_ref, cot_full.at[at(mine, columns), :], send_cot, recv_cot)
        copy.start()
        sent.append(copy)
    sent += begin(kvm, send_kv, recv_kv)
    sent += spread(counted, send_ct, recv_ct, 8)
    near_copies = [to_partner(0, k_ref), to_partner(1, v_ref), to_partner(2, q_ref)]
    near_copies[0].start()
    near_copies[1].start()
    cot_full[at(mine, columns), :] = cot_ref[...]
    for k in range(1, n_head):
        origin = lax.rem(mine + n_head - k, n_head)
        over_head(
            k, cot_ref, cot_full.at[at(origin, columns), :], send_cot, recv_cot
        ).wait_recv()
    sent += forward(kvm, send_kv, recv_kv)
    full = cot_full[...]
    grads[...] = product(w_ref[...], full, NN) * live_row
    for h in range(heads):
        both = jnp.concatenate([q_ref[hs(h), :], grads[hs(h), :]], axis=0)
        qdm[h, at(me, picked), :] = product(chooser[h], both, NT)
    sent += begin(qdm, send_qd, recv_qd)
    near_copies[2].start()
    near_grads = to_partner(3, grads)
    near_grads.start()

    finish(kvm, send_kv, recv_kv)
    gathered(counted, send_ct, recv_ct, 8)
    near_copies[0].wait_recv()
    near_copies[1].wait_recv()
    total = n_seq * picked
    slot = lax.broadcasted_iota(jnp.int32, (total, 1), 0) % picked
    counts_mid = jnp.concatenate(
        [jnp.broadcast_to(counted[0, 8 * i:8 * i + 1, 0:1], (picked, 1)) for i in range(n_seq)],
        axis=0,
    )
    partner_count = counted[0, at(partner, 8), :][0:1, 0:1]
    live_near = sub < partner_count

    kept = []
    stat_rows = []
    delta_rows = []
    for h in range(heads):
        o, far = offsets[h]
        place = SPACING_CENTRAL * slot + o
        far_slot = jnp.where(place % SPACING_WIDE == far, 1.0, 0.0)
        live_mid = jnp.where(place.astype(jnp.float32) < counts_mid, 1.0, 0.0)
        in_mid = jnp.where(lane % SPACING_CENTRAL == o, 1.0, 0.0)
        in_far = jnp.where(lane % SPACING_WIDE == far, 1.0, 0.0)
        times = live_mid * (in_mid + far_slot * in_far)
        q = q_ref[hs(h), :]
        d = grads[hs(h), :]
        km = kvm[h, :, 0:HEAD]
        vm = kvm[h, :, HEAD:2 * HEAD]
        k0, v0 = k_ref[hs(h), :], v_ref[hs(h), :]
        k1, v1 = near[0, hs(h), :], near[1, hs(h), :]
        sm = jnp.where(times > 0.5, product(km, q, NN) * scale, MASKED_SCORE)
        s0 = jnp.where(live_col, product(k0, q, TN) * scale, MASKED_SCORE)
        s1 = jnp.where(live_near, product(k1, q, TN) * scale, MASKED_SCORE)
        peak = jnp.maximum(
            jnp.max(sm, axis=0, keepdims=True),
            jnp.maximum(
                jnp.max(s0, axis=0, keepdims=True), jnp.max(s1, axis=0, keepdims=True)
            ),
        )
        wm = times * jnp.exp(sm - peak)
        w0 = jnp.exp(s0 - peak)
        w1 = jnp.exp(s1 - peak)
        bottom = (
            jnp.sum(wm, axis=0, keepdims=True)
            + jnp.sum(w0, axis=0, keepdims=True)
            + jnp.sum(w1, axis=0, keepdims=True)
        )
        inverse = 1.0 / bottom
        pm, p0, p1 = wm * inverse, w0 * inverse, w1 * inverse
        result = product(vm, pm, TN) + product(v0, p0, NN) + product(v1, p1, NN)
        lse = peak + jnp.log(bottom)
        delta = jnp.sum(d * result, axis=0, keepdims=True)
        attended[hs(h), :] = result * live_row
        stat_rows.append(lse)
        delta_rows.append(delta)
        kept.append((km, vm, pm, p0, p1, delta, far_slot, in_mid, in_far))
        if h == 0:
            sent += forward(qdm, send_qd, recv_qd)
    stat_slot = lax.broadcasted_iota(jnp.int32, (8, rows), 0)
    dense = jnp.zeros((8, rows), jnp.float32)
    for i, row in enumerate(stat_rows + delta_rows):
        dense = jnp.where(stat_slot == i, row, dense)
    stats[0, at(me, 8), :] = dense
    chunk = columns // n_seq
    local_w[...] = product(attended[...], full, NT)
    other = 1 - side

    def slab(part, k):
        return at(part * n_far + lax.rem(height + k, n_far), chunk)

    order = list(range(1, n_far)) + [0]
    for k in order:
        copy = beside(k, local_w.at[slab(other, k), :], w_half.at[k], send_y, recv_y)
        copy.start()
        sent.append(copy)
    sent += spread(stats, send_st, recv_st, 8)
    terms[...] = product(w_ref[...], attended[...], TN)
    for k in range(1, n_head):
        copy = over_head(
            k, terms.at[at(lax.rem(mine + k, n_head), columns), :], terms_in.at[k],
            send_o, recv_o,
        )
        copy.start()
        sent.append(copy)

    for k in order:
        beside(k, local_w.at[slab(side, k), :], w_half.at[k], send_y, recv_y).wait_recv()
        w_half[k] = w_half[k] + local_w[slab(side, k), :]
        if k > 0:
            copy = pltpu.make_async_remote_copy(
                src_ref=w_half.at[k], dst_ref=w_in.at[k], send_sem=send_w.at[k],
                recv_sem=recv_w.at[k], device_id={"seq": level(k)}, device_id_type=MESH,
            )
            copy.start()
            sent.append(copy)

    near_copies[2].wait_recv()
    for h in range(heads):
        km, vm, pm, p0, p1, delta, far_slot, in_mid, in_far = kept[h]
        d = grads[hs(h), :]
        q = q_ref[hs(h), :]
        k0, v0 = k_ref[hs(h), :], v_ref[hs(h), :]
        k1, v1 = near[0, hs(h), :], near[1, hs(h), :]
        gm = pm * (product(vm, d, NN) - delta)
        g0 = p0 * (product(v0, d, TN) - delta)
        g1 = p1 * (product(v1, d, TN) - delta)
        dq_ref[hs(h), :] = scale * (
            product(km, gm, TN) + product(k0, g0, NN) + product(k1, g1, NN)
        )
        dk_ref[hs(h), :] = product(q, g0, NT)
        dv_ref[hs(h), :] = product(d, p0, NT)

    summed = w_half[0]
    for k in range(1, n_far):
        pltpu.make_async_remote_copy(
            src_ref=w_half.at[k], dst_ref=w_in.at[k], send_sem=send_w.at[k],
            recv_sem=recv_w.at[k], device_id={"seq": level(k)}, device_id_type=MESH,
        ).wait_recv()
        summed = summed + w_in[k]
    dw_ref[slab(side, 0), :] = summed
    own_slab = dw_ref.at[slab(side, 0), :]
    starts = [across(k, own_slab, send_g, recv_g) for k in range(1, n_far)]
    starts.append(beside(0, own_slab, own_slab, send_g, recv_g))
    for copy in starts:
        copy.start()
    sent += starts

    finish(qdm, send_qd, recv_qd)
    gathered(stats, send_st, recv_st, 8)
    near_grads.wait_recv()
    def relay():
        for k in range(1, n_far):
            block = dw_ref.at[slab(side, n_far - k), :]
            across(k, block, send_g, recv_g).wait_recv()
            copy = beside(k, block, block, send_g, recv_g)
            copy.start()
            sent.append(copy)

    if heads < 2:
        relay()
    theirs = stats[0, at(partner, 8), :]
    for h in range(heads):
        _, _, _, _, _, _, far_slot, in_mid, in_far = kept[h]
        k0, v0 = k_ref[hs(h), :], v_ref[hs(h), :]
        q1, d1 = near[2, hs(h), :], near[3, hs(h), :]
        lse1 = theirs[h:h + 1, :]
        delta1 = theirs[heads + h:heads + h + 1, :]
        sx = jnp.where(live_col, product(k0, q1, TN) * scale, MASKED_SCORE)
        px = jnp.exp(sx - lse1)
        gx = px * (product(v0, d1, TN) - delta1)
        qm = qdm[h, :, 0:HEAD]
        dm = qdm[h, :, HEAD:2 * HEAD]
        times = live_row * (in_mid + far_slot * in_far)
        sy = jnp.where(times > 0.5, product(qm, k0, NN) * scale, MASKED_SCORE)
        lse_col, delta_col = [
            jnp.concatenate(
                [
                    jnp.sum(chooser[h] * stats[0, 8 * i + j:8 * i + j + 1, :], axis=1, keepdims=True)
                    for i in range(n_seq)
                ],
                axis=0,
            )
            for j in (h, heads + h)
        ]
        py = times * jnp.exp(sy - lse_col)
        gy = py * (product(dm, v0, NN) - delta_col)
        dk_ref[hs(h), :] = scale * (
            dk_ref[hs(h), :] + product(q1, gx, NT) + product(qm, gy, TN)
        )
        dv_ref[hs(h), :] = dv_ref[hs(h), :] + product(d1, px, NT) + product(dm, py, TN)
        if h == heads - 2:
            relay()

    output = terms[at(mine, columns), :]
    for k in range(1, n_head):
        over_head(
            k, terms.at[at(mine, columns), :], terms_in.at[k], send_o, recv_o
        ).wait_recv()
    for k in range(1, n_head):
        output = output + terms_in[k]
    out_ref[...] = output
    for k in range(n_far):
        block = dw_ref.at[slab(other, n_far - k), :]
        beside(k, block, block, send_g, recv_g).wait_recv()
    for copy in near_copies + [near_grads] + sent:
        copy.wait_send()


def settle_kernel(*refs):
    count = (len(refs) - 2) // 3
    load_sem, store_sem = refs[-2:]
    held = refs[2 * count:3 * count]
    loads = [
        pltpu.make_async_copy(refs[i], held[i], load_sem.at[i]) for i in range(count)
    ]
    stores = [
        pltpu.make_async_copy(held[i], refs[count + i], store_sem.at[i]) for i in range(count)
    ]
    for load in loads:
        load.start()
    for load, store in zip(loads, stores):
        load.wait()
        store.start()
    for store in stores:
        store.wait()


def settle(arrays):
    hbm = pl.BlockSpec(memory_space=pltpu.MemorySpace.HBM)
    return pl.pallas_call(
        settle_kernel,
        out_shape=tuple(jax.ShapeDtypeStruct(a.shape, a.dtype) for a in arrays),
        in_specs=[hbm] * len(arrays),
        out_specs=(hbm,) * len(arrays),
        scratch_shapes=[pltpu.VMEM(a.shape, a.dtype) for a in arrays]
        + [pltpu.SemaphoreType.DMA((len(arrays),))] * 2,
        compiler_params=pltpu.CompilerParams(vmem_limit_bytes=60 * 1024 * 1024),
    )(*arrays)


def fused(n_seq, n_head, queries, keys, values, counts, out_weight, cotangent):
    columns, rows = queries.shape
    wide = out_weight.shape[1]
    heads = columns // HEAD
    picked = rows // SPACING_CENTRAL
    chunk = columns // n_seq
    block = jax.ShapeDtypeStruct((columns, rows), jnp.float32)
    vmem = pl.BlockSpec(memory_space=pltpu.VMEM)
    hbm = pl.BlockSpec(memory_space=pltpu.MemorySpace.HBM)
    f32 = jnp.float32
    seq_sem = pltpu.SemaphoreType.DMA((n_seq,))
    head_sem = pltpu.SemaphoreType.DMA((n_head,))
    near_sem = pltpu.SemaphoreType.DMA((4,))
    results = pl.pallas_call(
        functools.partial(fused_kernel, n_seq, n_head),
        out_shape=(block, block, block, block, jax.ShapeDtypeStruct((columns, wide), f32)),
        in_specs=[hbm, hbm, hbm, pl.BlockSpec(memory_space=pltpu.SMEM), hbm, hbm],
        out_specs=(vmem,) * 5,
        scratch_shapes=[
            pltpu.VMEM((columns, rows), f32),
            pltpu.VMEM((columns, rows), f32),
            pltpu.VMEM((columns, rows), f32),
            pltpu.VMEM((columns, wide), f32),
            pltpu.VMEM((columns, rows), f32),
            pltpu.SemaphoreType.DMA((5,)),
            pltpu.VMEM((1, n_seq * 8, rows), f32),
            seq_sem, seq_sem, seq_sem, seq_sem,
            pltpu.VMEM((n_seq // 2, chunk, wide), f32),
            pltpu.VMEM((columns * n_head, rows), f32),
            pltpu.VMEM((4, columns, rows), f32),
            pltpu.VMEM((columns, rows), f32),
            pltpu.VMEM((heads, n_seq * picked, rows), f32),
            pltpu.VMEM((heads, n_seq * picked, rows), f32),
            pltpu.VMEM((1, n_seq * 8, rows), f32),
            pltpu.VMEM((columns, rows), f32),
            pltpu.VMEM((wide, rows), f32),
            pltpu.VMEM((n_head, columns, rows), f32),
            pltpu.VMEM((columns, wide), f32),
            pltpu.VMEM((n_seq // 2, chunk, wide), f32),
            head_sem, head_sem, near_sem, near_sem, seq_sem, seq_sem, seq_sem, seq_sem,
            seq_sem, seq_sem, seq_sem, seq_sem, seq_sem, seq_sem, head_sem, head_sem,
        ],
        compiler_params=pltpu.CompilerParams(
            collective_id=0, has_side_effects=True, vmem_limit_bytes=60 * 1024 * 1024
        ),
    )(queries, keys, values, counts, out_weight, cotangent)
    return settle(results)


def solution(mesh):
    n_seq, n_head = mesh.shape["seq"], mesh.shape["head"]
    whole_is_middle = n_seq <= 1 << LOG2_CENTRAL and n_seq % 2 == 0
    body = functools.partial(fused, n_seq, n_head) if whole_is_middle else on_device
    in_specs = (
        P("head", "seq"),
        P("head", "seq"),
        P("head", "seq"),
        P("seq"),
        P("head", None),
        P("head", "seq"),
    )
    out_specs = (
        P("head", "seq"),
        P("head", "seq"),
        P("head", "seq"),
        P("head", "seq"),
        P("head", None),
    )
    return jax.shard_map(
        body, mesh=mesh, in_specs=in_specs, out_specs=out_specs, check_vma=False
    )
```

```python
import functools

import jax
import jax.numpy as jnp
from jax import lax
from jax.experimental import pallas as pl
from jax.experimental.pallas import tpu as pltpu
from jax.sharding import PartitionSpec as P

HEAD = 64
SPACING_LOCAL = 1
SPACING_CENTRAL = 4
SPACING_WIDE = 16
LOG2_LOCAL = 1
LOG2_CENTRAL = 4


PRECISE = lax.Precision.HIGHEST
MASKED_SCORE = -1e30


def from_partner(shard, axis, apart):
    return lax.ppermute(shard, axis, [(i, i ^ 1 << apart) for i in range(lax.axis_size(axis))])


def pick_rows(block, chooser):
    spacing = chooser.shape[1]
    if spacing == 1:
        return block
    shaped = block.reshape(block.shape[:-1] + (block.shape[-1] // spacing, spacing))
    factor = chooser.reshape((chooser.shape[0],) + (1,) * (block.ndim - 1) + (spacing,))
    return jnp.sum(shaped * factor, axis=-1)


def place_rows(piece, chooser, filler):
    spacing = chooser.shape[1]
    if spacing == 1:
        return piece
    chosen = (chooser > 0.5).reshape((chooser.shape[0],) + (1,) * (piece.ndim - 1) + (spacing,))
    spread = jnp.where(chosen, piece[..., None], filler)
    return spread.reshape(piece.shape[:-1] + (piece.shape[-1] * spacing,))


def scores_of(query_rows, key_rows, key_live, score_scale):
    raw = jnp.einsum("heq,hek->hqk", query_rows, key_rows, precision=PRECISE) * score_scale
    return jnp.where(key_live[:, None, :] > 0.5, raw, MASKED_SCORE)


def segment_rows(bundle, extras, levels):
    for bit_index in range(levels):
        other_bundle, other_extras = from_partner((bundle, extras), "seq", bit_index)
        bundle = jnp.concatenate([bundle, other_bundle], axis=3)
        extras = jnp.concatenate([extras, other_extras], axis=3)
    return (bundle, extras)


def return_terms(terms, levels):
    for bit_index in reversed(range(levels)):
        half = terms.shape[3] // 2
        arrived = from_partner(terms[:, :, :, half:], "seq", bit_index)
        terms = terms[:, :, :, :half] + arrived
    return terms


def key_side(key_own, value_own, own_live, far_query, far_grad, far_lse, far_delta, score_scale):
    scores = scores_of(far_query, key_own, own_live, score_scale)
    probabilities = jnp.exp(scores - far_lse[:, :, None])
    value_part = jnp.einsum("hqk,heq->hek", probabilities, far_grad, precision=PRECISE)
    prob_grads = jnp.einsum("heq,hek->hqk", far_grad, value_own, precision=PRECISE)
    score_grads = probabilities * (prob_grads - far_delta[:, :, None])
    key_part = score_scale * jnp.einsum("hqk,heq->hek", score_grads, far_query, precision=PRECISE)
    return (key_part, value_part)


def segment_grads_of(query_rows, grad_rows, probabilities, score_grads, levels, score_scale):
    key_terms = score_scale * jnp.einsum("hqk,heq->hek", score_grads, query_rows, precision=PRECISE)
    value_terms = jnp.einsum("hqk,heq->hek", probabilities, grad_rows, precision=PRECISE)
    owned = return_terms(jnp.stack([key_terms, value_terms]), levels)
    return (owned[0], owned[1])


def on_device(queries, keys, values, counts, out_weight, cotangent):
    columns, row_count = queries.shape
    local_heads = columns // HEAD
    score_scale = HEAD ** (-0.5)
    shard_levels = lax.axis_size("seq").bit_length() - 1
    branches = (
        (SPACING_LOCAL, min(LOG2_LOCAL, shard_levels)),
        (SPACING_CENTRAL, min(LOG2_CENTRAL, shard_levels)),
    )
    global_heads = lax.axis_index("head") * local_heads + jnp.arange(local_heads, dtype=jnp.int32)
    active_rows = (jnp.arange(row_count, dtype=jnp.int32) < counts[0]).astype(jnp.float32)
    live_heads = jnp.broadcast_to(active_rows[None, :], (local_heads, row_count))
    q_all = queries.reshape(local_heads, HEAD, row_count)
    k_all = keys.reshape(local_heads, HEAD, row_count)
    v_all = values.reshape(local_heads, HEAD, row_count)

    def chooser_for(spacing):
        offsets = global_heads % spacing
        return (jnp.arange(spacing, dtype=jnp.int32)[None, :] == offsets[:, None]).astype(
            jnp.float32
        )

    remembered = []
    out_list = []
    lse_list = []
    for spacing_factor, levels in branches:
        chooser = chooser_for(spacing_factor)
        query_rows = pick_rows(q_all, chooser)
        key_own = pick_rows(k_all, chooser)
        value_own = pick_rows(v_all, chooser)
        own_live = pick_rows(live_heads, chooser)
        pairs, extras = segment_rows(
            jnp.stack([key_own, value_own]), own_live[None, :, None, :], levels
        )
        key_rows = pairs[0]
        value_rows = pairs[1]
        key_live = extras[0, :, 0, :]
        scores = scores_of(query_rows, key_rows, key_live, score_scale)
        row_max = jnp.max(scores, axis=-1)
        weights = jnp.exp(scores - row_max[..., None])
        denominator = jnp.sum(weights, axis=-1)
        branch_out = (
            jnp.einsum("hqk,hek->heq", weights, value_rows, precision=PRECISE)
            / denominator[:, None, :]
        )
        log_total = row_max + jnp.log(denominator)
        out_list.append(place_rows(branch_out, chooser, 0.0))
        lse_list.append(place_rows(log_total, chooser, MASKED_SCORE))
        remembered.append(
            (
                chooser,
                levels,
                query_rows,
                key_own,
                value_own,
                own_live,
                key_rows,
                value_rows,
                key_live,
            )
        )
    far_chooser = chooser_for(SPACING_WIDE)
    far_query = pick_rows(q_all, far_chooser)
    far_key = pick_rows(k_all, far_chooser)
    far_value = pick_rows(v_all, far_chooser)
    far_live = pick_rows(live_heads, far_chooser)
    far_pairs = jnp.stack([far_key, far_value])
    far_extras = far_live[None, :, None, :]
    far_rows = far_query.shape[2]
    running_max = jnp.full((local_heads, far_rows), MASKED_SCORE, jnp.float32)
    pairs_piece = lax.all_gather(far_pairs, "seq", axis=3, tiled=True)
    extras_piece = lax.all_gather(far_extras, "seq", axis=3, tiled=True)
    absorb_scores = scores_of(far_query, pairs_piece[0], extras_piece[0, :, 0, :], score_scale)
    newest = jnp.maximum(running_max, jnp.max(absorb_scores, axis=-1))
    weights = jnp.exp(absorb_scores - newest[..., None])
    summed = jnp.sum(weights, axis=-1)
    gathered = jnp.einsum("hqk,hek->heq", weights, pairs_piece[1], precision=PRECISE)
    out_list.append(place_rows(gathered / summed[:, None, :], far_chooser, 0.0))
    lse_list.append(place_rows(newest + jnp.log(summed), far_chooser, MASKED_SCORE))
    stacked = jnp.stack(lse_list)
    row_peak = jnp.max(stacked, axis=0)
    combined_lse = row_peak + jnp.log(jnp.sum(jnp.exp(stacked - row_peak[None]), axis=0))
    combined = jnp.zeros((local_heads, HEAD, row_count), jnp.float32)
    for spread_lse, spread_out in zip(lse_list, out_list):
        combined = combined + jnp.exp(spread_lse - combined_lse)[:, None, :] * spread_out
    attended = (combined * active_rows[None, None, :]).reshape(columns, row_count)
    terms = lax.dot_general(
        out_weight,
        attended,
        (((0,), (0,)), ((), ())),
        precision=PRECISE,
        preferred_element_type=jnp.float32,
    )
    output = lax.psum_scatter(terms, "head", scatter_dimension=0, tiled=True)
    full_grad = lax.all_gather(cotangent, "head", axis=0, tiled=True)
    grad_attended = jnp.dot(
        out_weight, full_grad, precision=PRECISE, preferred_element_type=jnp.float32
    )
    weight_local = lax.dot_general(
        attended,
        full_grad,
        (((1,), (1,)), ((), ())),
        precision=PRECISE,
        preferred_element_type=jnp.float32,
    )
    weight_grad = lax.psum(weight_local, "seq")
    grad_all = grad_attended.reshape(local_heads, HEAD, row_count) * active_rows[None, None, :]
    delta_all = jnp.sum(grad_all * combined, axis=1)
    query_grad = jnp.zeros((local_heads, HEAD, row_count), jnp.float32)
    key_grad = jnp.zeros((local_heads, HEAD, row_count), jnp.float32)
    value_grad = jnp.zeros((local_heads, HEAD, row_count), jnp.float32)
    for (
        chooser,
        levels,
        query_rows,
        key_own,
        value_own,
        own_live,
        key_rows,
        value_rows,
        key_live,
    ) in remembered:
        grad_rows = pick_rows(grad_all, chooser)
        lse_rows = pick_rows(combined_lse, chooser)
        delta_rows = pick_rows(delta_all, chooser)
        scores = scores_of(query_rows, key_rows, key_live, score_scale)
        probabilities = jnp.exp(scores - lse_rows[:, :, None])
        prob_grads = jnp.einsum("heq,hek->hqk", grad_rows, value_rows, precision=PRECISE)
        score_grads = probabilities * (prob_grads - delta_rows[:, :, None])
        query_part = score_scale * jnp.einsum(
            "hqk,hek->heq", score_grads, key_rows, precision=PRECISE
        )
        key_part, value_part = segment_grads_of(
            query_rows, grad_rows, probabilities, score_grads, levels, score_scale
        )
        query_grad = query_grad + place_rows(query_part, chooser, 0.0)
        key_grad = key_grad + place_rows(key_part, chooser, 0.0)
        value_grad = value_grad + place_rows(value_part, chooser, 0.0)
    far_grad = pick_rows(grad_all, far_chooser)
    far_lse = pick_rows(combined_lse, far_chooser)
    far_delta = pick_rows(delta_all, far_chooser)
    pairs_piece = lax.all_gather(far_pairs, "seq", axis=3, tiled=True)
    extras_piece = lax.all_gather(far_extras, "seq", axis=3, tiled=True)
    scores = scores_of(far_query, pairs_piece[0], extras_piece[0, :, 0, :], score_scale)
    probabilities = jnp.exp(scores - far_lse[:, :, None])
    prob_grads = jnp.einsum("heq,hek->hqk", far_grad, pairs_piece[1], precision=PRECISE)
    score_grads = probabilities * (prob_grads - far_delta[:, :, None])
    far_query_part = score_scale * jnp.einsum(
        "hqk,hek->heq", score_grads, pairs_piece[0], precision=PRECISE
    )
    far_bundle = jnp.stack([far_query, far_grad])
    far_stats = jnp.stack([far_lse, far_delta])[:, :, None, :]
    bundle_piece = lax.all_gather(far_bundle, "seq", axis=3, tiled=True)
    stats_piece = lax.all_gather(far_stats, "seq", axis=3, tiled=True)
    key_part, value_part = key_side(
        far_key,
        far_value,
        far_live,
        bundle_piece[0],
        bundle_piece[1],
        stats_piece[0, :, 0, :],
        stats_piece[1, :, 0, :],
        score_scale,
    )
    query_grad = query_grad + place_rows(far_query_part, far_chooser, 0.0)
    key_grad = key_grad + place_rows(key_part, far_chooser, 0.0)
    value_grad = value_grad + place_rows(value_part, far_chooser, 0.0)
    return (
        output,
        query_grad.reshape(columns, row_count),
        key_grad.reshape(columns, row_count),
        value_grad.reshape(columns, row_count),
        weight_grad,
    )


MESH = pl.DeviceIdType.MESH
NN = ((1,), (0,))
TN = ((0,), (0,))
NT = ((1,), (1,))


def product(a, b, dims):
    def once(x, y):
        return lax.dot_general(
            x, y, (dims, ((), ())), preferred_element_type=jnp.float32
        )

    a_top, b_top = a.astype(jnp.bfloat16), b.astype(jnp.bfloat16)
    a_rest = (a - a_top.astype(jnp.float32)).astype(jnp.bfloat16)
    b_rest = (b - b_top.astype(jnp.float32)).astype(jnp.bfloat16)
    return once(a_top, b_top) + (once(a_top, b_rest) + once(a_rest, b_top))


def fused_kernel(
    n_seq, n_head,
    q_hbm, k_hbm, v_hbm, count_ref, w_hbm, cot_hbm,
    out_ref, dq_ref, dk_ref, dv_ref, dw_ref,
    q_ref, k_ref, v_ref, w_ref, cot_ref, load_sem, counted, send_ct, recv_ct, send_y, recv_y, w_half,
    cot_full, near, grads, kvm, qdm, stats, attended, terms, terms_in, local_w, w_in,
    send_cot, recv_cot, send_near, recv_near, send_kv, recv_kv, send_qd, recv_qd,
    send_st, recv_st, send_w, recv_w, send_g, recv_g, send_o, recv_o,
):
    columns, rows = q_ref.shape
    heads = columns // HEAD
    picked = rows // SPACING_CENTRAL
    n_far = n_seq // 2
    loads = [
        pltpu.make_async_copy(src, dst, load_sem.at[i])
        for i, (src, dst) in enumerate(
            ((k_hbm, k_ref), (v_hbm, v_ref), (cot_hbm, cot_ref), (q_hbm, q_ref), (w_hbm, w_ref))
        )
    ]
    for load in loads:
        load.start()
    scale = HEAD ** (-0.5)
    me = lax.axis_index("seq")
    mine = lax.axis_index("head")
    side, height = me % 2, me // 2
    partner = me + 1 - 2 * side

    def at(start, size):
        return pl.ds(pl.multiple_of(start * size, size), size)

    barrier = pltpu.get_barrier_semaphore()
    for k in range(1, n_seq):
        pl.semaphore_signal(
            barrier, inc=1, device_id={"seq": lax.rem(me + k, n_seq)}, device_id_type=MESH
        )
    for k in range(1, n_head):
        pl.semaphore_signal(
            barrier, inc=1, device_id={"head": lax.rem(mine + k, n_head)}, device_id_type=MESH
        )
    offsets = []
    for h in range(heads):
        g = mine * heads + h
        offsets.append((g % SPACING_CENTRAL, g % SPACING_WIDE))
    pick_row = lax.broadcasted_iota(jnp.int32, (picked, rows), 0)
    pick_col = lax.broadcasted_iota(jnp.int32, (picked, rows), 1)
    chooser = [
        jnp.where(pick_col == SPACING_CENTRAL * pick_row + o, 1.0, 0.0) for o, _ in offsets
    ]
    count = jnp.full((picked, rows), count_ref[0], jnp.int32).astype(jnp.float32)
    lane = lax.broadcasted_iota(jnp.int32, (1, rows), 1)
    sub = lax.broadcasted_iota(jnp.int32, (rows, 1), 0).astype(jnp.float32)
    live_row = jnp.where(lane.astype(jnp.float32) < count[0:1, :], 1.0, 0.0)
    live_col = sub < count[0:1, 0:1]

    def hs(h):
        return slice(h * HEAD, (h + 1) * HEAD)

    loads[0].wait()
    loads[1].wait()
    for h in range(heads):
        both = jnp.concatenate([k_ref[hs(h), :], v_ref[hs(h), :]], axis=0)
        kvm[h, at(me, picked), :] = product(chooser[h], both, NT)
    counted[0, at(me, 8), :] = count[0:8, :]
    loads[2].wait()
    loads[3].wait()
    loads[4].wait()
    pl.semaphore_wait(barrier, n_seq + n_head - 2)

    def over_seq(k, src, dst, send, recv):
        return pltpu.make_async_remote_copy(
            src_ref=src, dst_ref=dst, send_sem=send.at[k], recv_sem=recv.at[k],
            device_id={"seq": lax.rem(me + k, n_seq)}, device_id_type=MESH,
        )

    def over_head(k, src, dst, send, recv):
        return pltpu.make_async_remote_copy(
            src_ref=src, dst_ref=dst, send_sem=send.at[k], recv_sem=recv.at[k],
            device_id={"head": lax.rem(mine + k, n_head)}, device_id_type=MESH,
        )

    def to_partner(k, src):
        return pltpu.make_async_remote_copy(
            src_ref=src, dst_ref=near.at[k], send_sem=send_near.at[k],
            recv_sem=recv_near.at[k], device_id={"seq": partner}, device_id_type=MESH,
        )

    def source(k):
        return lax.rem(me + n_seq - k, n_seq)

    def spread(buffer, send, recv, size):
        out = []
        for k in range(1, n_seq):
            block = buffer.at[:, at(me, size), :]
            copy = over_seq(k, block, block, send, recv)
            copy.start()
            out.append(copy)
        return out

    def gathered(buffer, send, recv, size):
        for k in range(1, n_seq):
            block = buffer.at[:, at(source(k), size), :]
            over_seq(k, block, block, send, recv).wait_recv()

    def level(k):
        return 2 * lax.rem(height + k, n_far) + side

    def level_from(k):
        return 2 * lax.rem(height + n_far - k, n_far) + side

    def across(k, block, send, recv):
        return pltpu.make_async_remote_copy(
            src_ref=block, dst_ref=block, send_sem=send.at[k], recv_sem=recv.at[k],
            device_id={"seq": level(k)}, device_id_type=MESH,
        )

    def beside(k, src, dst, send, recv):
        return pltpu.make_async_remote_copy(
            src_ref=src, dst_ref=dst, send_sem=send.at[n_far + k], recv_sem=recv.at[n_far + k],
            device_id={"seq": partner}, device_id_type=MESH,
        )

    def piece(buffer, owner):
        return buffer.at[:, at(owner, picked), :]

    def begin(buffer, send, recv):
        own = piece(buffer, me)
        out = [across(k, own, send, recv) for k in range(1, n_far)]
        out.append(beside(0, own, own, send, recv))
        for copy in out:
            copy.start()
        return out

    def forward(buffer, send, recv):
        out = []
        for k in range(1, n_far):
            block = piece(buffer, level_from(k))
            across(k, block, send, recv).wait_recv()
            copy = beside(k, block, block, send, recv)
            copy.start()
            out.append(copy)
        return out

    def finish(buffer, send, recv):
        for k in range(n_far):
            owner = level_from(k) + 1 - 2 * side
            block = piece(buffer, owner)
            beside(k, block, block, send, recv).wait_recv()

    sent = []
    for k in range(1, n_head):
        copy = over_head(k, cot_ref, cot_full.at[at(mine, columns), :], send_cot, recv_cot)
        copy.start()
        sent.append(copy)
    sent += begin(kvm, send_kv, recv_kv)
    sent += spread(counted, send_ct, recv_ct, 8)
    near_copies = [to_partner(0, k_ref), to_partner(1, v_ref), to_partner(2, q_ref)]
    near_copies[0].start()
    near_copies[1].start()
    cot_full[at(mine, columns), :] = cot_ref[...]
    for k in range(1, n_head):
        origin = lax.rem(mine + n_head - k, n_head)
        over_head(
            k, cot_ref, cot_full.at[at(origin, columns), :], send_cot, recv_cot
        ).wait_recv()
    sent += forward(kvm, send_kv, recv_kv)
    full = cot_full[...]
    grads[...] = product(w_ref[...], full, NN) * live_row
    for h in range(heads):
        both = jnp.concatenate([q_ref[hs(h), :], grads[hs(h), :]], axis=0)
        qdm[h, at(me, picked), :] = product(chooser[h], both, NT)
    sent += begin(qdm, send_qd, recv_qd)
    near_copies[2].start()
    near_grads = to_partner(3, grads)
    near_grads.start()

    finish(kvm, send_kv, recv_kv)
    gathered(counted, send_ct, recv_ct, 8)
    near_copies[0].wait_recv()
    near_copies[1].wait_recv()
    total = n_seq * picked
    slot = lax.broadcasted_iota(jnp.int32, (total, 1), 0) % picked
    counts_mid = jnp.concatenate(
        [jnp.broadcast_to(counted[0, 8 * i:8 * i + 1, 0:1], (picked, 1)) for i in range(n_seq)],
        axis=0,
    )
    partner_count = counted[0, at(partner, 8), :][0:1, 0:1]
    live_near = sub < partner_count

    kept = []
    stat_rows = []
    delta_rows = []
    for h in range(heads):
        o, far = offsets[h]
        place = SPACING_CENTRAL * slot + o
        far_slot = jnp.where(place % SPACING_WIDE == far, 1.0, 0.0)
        live_mid = jnp.where(place.astype(jnp.float32) < counts_mid, 1.0, 0.0)
        in_mid = jnp.where(lane % SPACING_CENTRAL == o, 1.0, 0.0)
        in_far = jnp.where(lane % SPACING_WIDE == far, 1.0, 0.0)
        times = live_mid * (in_mid + far_slot * in_far)
        q = q_ref[hs(h), :]
        d = grads[hs(h), :]
        km = kvm[h, :, 0:HEAD]
        vm = kvm[h, :, HEAD:2 * HEAD]
        k0, v0 = k_ref[hs(h), :], v_ref[hs(h), :]
        k1, v1 = near[0, hs(h), :], near[1, hs(h), :]
        sm = jnp.where(times > 0.5, product(km, q, NN) * scale, MASKED_SCORE)
        s0 = jnp.where(live_col, product(k0, q, TN) * scale, MASKED_SCORE)
        s1 = jnp.where(live_near, product(k1, q, TN) * scale, MASKED_SCORE)
        peak = jnp.maximum(
            jnp.max(sm, axis=0, keepdims=True),
            jnp.maximum(
                jnp.max(s0, axis=0, keepdims=True), jnp.max(s1, axis=0, keepdims=True)
            ),
        )
        wm = times * jnp.exp(sm - peak)
        w0 = jnp.exp(s0 - peak)
        w1 = jnp.exp(s1 - peak)
        bottom = (
            jnp.sum(wm, axis=0, keepdims=True)
            + jnp.sum(w0, axis=0, keepdims=True)
            + jnp.sum(w1, axis=0, keepdims=True)
        )
        inverse = 1.0 / bottom
        pm, p0, p1 = wm * inverse, w0 * inverse, w1 * inverse
        result = product(vm, pm, TN) + product(v0, p0, NN) + product(v1, p1, NN)
        lse = peak + jnp.log(bottom)
        delta = jnp.sum(d * result, axis=0, keepdims=True)
        attended[hs(h), :] = result * live_row
        stat_rows.append(lse)
        delta_rows.append(delta)
        kept.append((km, vm, pm, p0, p1, delta, far_slot, in_mid, in_far))
    stat_slot = lax.broadcasted_iota(jnp.int32, (8, rows), 0)
    dense = jnp.zeros((8, rows), jnp.float32)
    for i, row in enumerate(stat_rows + delta_rows):
        dense = jnp.where(stat_slot == i, row, dense)
    stats[0, at(me, 8), :] = dense
    chunk = columns // n_seq
    local_w[...] = product(attended[...], full, NT)
    other = 1 - side

    def slab(part, k):
        return at(part * n_far + lax.rem(height + k, n_far), chunk)

    order = list(range(1, n_far)) + [0]
    for k in order:
        copy = beside(k, local_w.at[slab(other, k), :], w_half.at[k], send_y, recv_y)
        copy.start()
        sent.append(copy)
    sent += spread(stats, send_st, recv_st, 8)
    sent += forward(qdm, send_qd, recv_qd)
    terms[...] = product(w_ref[...], attended[...], TN)
    for k in range(1, n_head):
        copy = over_head(
            k, terms.at[at(lax.rem(mine + k, n_head), columns), :], terms_in.at[k],
            send_o, recv_o,
        )
        copy.start()
        sent.append(copy)

    for k in order:
        beside(k, local_w.at[slab(side, k), :], w_half.at[k], send_y, recv_y).wait_recv()
        w_half[k] = w_half[k] + local_w[slab(side, k), :]
        if k > 0:
            copy = pltpu.make_async_remote_copy(
                src_ref=w_half.at[k], dst_ref=w_in.at[k], send_sem=send_w.at[k],
                recv_sem=recv_w.at[k], device_id={"seq": level(k)}, device_id_type=MESH,
            )
            copy.start()
            sent.append(copy)

    near_copies[2].wait_recv()
    for h in range(heads):
        km, vm, pm, p0, p1, delta, far_slot, in_mid, in_far = kept[h]
        d = grads[hs(h), :]
        q = q_ref[hs(h), :]
        k0, v0 = k_ref[hs(h), :], v_ref[hs(h), :]
        k1, v1 = near[0, hs(h), :], near[1, hs(h), :]
        gm = pm * (product(vm, d, NN) - delta)
        g0 = p0 * (product(v0, d, TN) - delta)
        g1 = p1 * (product(v1, d, TN) - delta)
        dq_ref[hs(h), :] = scale * (
            product(km, gm, TN) + product(k0, g0, NN) + product(k1, g1, NN)
        )
        dk_ref[hs(h), :] = product(q, g0, NT)
        dv_ref[hs(h), :] = product(d, p0, NT)

    summed = w_half[0]
    for k in range(1, n_far):
        pltpu.make_async_remote_copy(
            src_ref=w_half.at[k], dst_ref=w_in.at[k], send_sem=send_w.at[k],
            recv_sem=recv_w.at[k], device_id={"seq": level(k)}, device_id_type=MESH,
        ).wait_recv()
        summed = summed + w_in[k]
    dw_ref[slab(side, 0), :] = summed
    own_slab = dw_ref.at[slab(side, 0), :]
    starts = [across(k, own_slab, send_g, recv_g) for k in range(1, n_far)]
    starts.append(beside(0, own_slab, own_slab, send_g, recv_g))
    for copy in starts:
        copy.start()
    sent += starts

    finish(qdm, send_qd, recv_qd)
    gathered(stats, send_st, recv_st, 8)
    near_grads.wait_recv()
    def relay():
        for k in range(1, n_far):
            block = dw_ref.at[slab(side, n_far - k), :]
            across(k, block, send_g, recv_g).wait_recv()
            copy = beside(k, block, block, send_g, recv_g)
            copy.start()
            sent.append(copy)

    if heads < 2:
        relay()
    theirs = stats[0, at(partner, 8), :]
    for h in range(heads):
        _, _, _, _, _, _, far_slot, in_mid, in_far = kept[h]
        k0, v0 = k_ref[hs(h), :], v_ref[hs(h), :]
        q1, d1 = near[2, hs(h), :], near[3, hs(h), :]
        lse1 = theirs[h:h + 1, :]
        delta1 = theirs[heads + h:heads + h + 1, :]
        sx = jnp.where(live_col, product(k0, q1, TN) * scale, MASKED_SCORE)
        px = jnp.exp(sx - lse1)
        gx = px * (product(v0, d1, TN) - delta1)
        qm = qdm[h, :, 0:HEAD]
        dm = qdm[h, :, HEAD:2 * HEAD]
        times = live_row * (in_mid + far_slot * in_far)
        sy = jnp.where(times > 0.5, product(qm, k0, NN) * scale, MASKED_SCORE)
        lse_col, delta_col = [
            jnp.concatenate(
                [
                    jnp.sum(chooser[h] * stats[0, 8 * i + j:8 * i + j + 1, :], axis=1, keepdims=True)
                    for i in range(n_seq)
                ],
                axis=0,
            )
            for j in (h, heads + h)
        ]
        py = times * jnp.exp(sy - lse_col)
        gy = py * (product(dm, v0, NN) - delta_col)
        dk_ref[hs(h), :] = scale * (
            dk_ref[hs(h), :] + product(q1, gx, NT) + product(qm, gy, TN)
        )
        dv_ref[hs(h), :] = dv_ref[hs(h), :] + product(d1, px, NT) + product(dm, py, TN)
        if h == heads - 2:
            relay()

    output = terms[at(mine, columns), :]
    for k in range(1, n_head):
        over_head(
            k, terms.at[at(mine, columns), :], terms_in.at[k], send_o, recv_o
        ).wait_recv()
    for k in range(1, n_head):
        output = output + terms_in[k]
    out_ref[...] = output
    for k in range(n_far):
        block = dw_ref.at[slab(other, n_far - k), :]
        beside(k, block, block, send_g, recv_g).wait_recv()
    for copy in near_copies + [near_grads] + sent:
        copy.wait_send()


def settle_kernel(*refs):
    count = (len(refs) - 2) // 3
    load_sem, store_sem = refs[-2:]
    held = refs[2 * count:3 * count]
    loads = [
        pltpu.make_async_copy(refs[i], held[i], load_sem.at[i]) for i in range(count)
    ]
    stores = [
        pltpu.make_async_copy(held[i], refs[count + i], store_sem.at[i]) for i in range(count)
    ]
    for load in loads:
        load.start()
    for load, store in zip(loads, stores):
        load.wait()
        store.start()
    for store in stores:
        store.wait()


def settle(arrays):
    hbm = pl.BlockSpec(memory_space=pltpu.MemorySpace.HBM)
    return pl.pallas_call(
        settle_kernel,
        out_shape=tuple(jax.ShapeDtypeStruct(a.shape, a.dtype) for a in arrays),
        in_specs=[hbm] * len(arrays),
        out_specs=(hbm,) * len(arrays),
        scratch_shapes=[pltpu.VMEM(a.shape, a.dtype) for a in arrays]
        + [pltpu.SemaphoreType.DMA((len(arrays),))] * 2,
        compiler_params=pltpu.CompilerParams(vmem_limit_bytes=60 * 1024 * 1024),
    )(*arrays)


def fused(n_seq, n_head, queries, keys, values, counts, out_weight, cotangent):
    columns, rows = queries.shape
    wide = out_weight.shape[1]
    heads = columns // HEAD
    picked = rows // SPACING_CENTRAL
    chunk = columns // n_seq
    block = jax.ShapeDtypeStruct((columns, rows), jnp.float32)
    vmem = pl.BlockSpec(memory_space=pltpu.VMEM)
    hbm = pl.BlockSpec(memory_space=pltpu.MemorySpace.HBM)
    f32 = jnp.float32
    seq_sem = pltpu.SemaphoreType.DMA((n_seq,))
    head_sem = pltpu.SemaphoreType.DMA((n_head,))
    near_sem = pltpu.SemaphoreType.DMA((4,))
    results = pl.pallas_call(
        functools.partial(fused_kernel, n_seq, n_head),
        out_shape=(block, block, block, block, jax.ShapeDtypeStruct((columns, wide), f32)),
        in_specs=[hbm, hbm, hbm, pl.BlockSpec(memory_space=pltpu.SMEM), hbm, hbm],
        out_specs=(vmem,) * 5,
        scratch_shapes=[
            pltpu.VMEM((columns, rows), f32),
            pltpu.VMEM((columns, rows), f32),
            pltpu.VMEM((columns, rows), f32),
            pltpu.VMEM((columns, wide), f32),
            pltpu.VMEM((columns, rows), f32),
            pltpu.SemaphoreType.DMA((5,)),
            pltpu.VMEM((1, n_seq * 8, rows), f32),
            seq_sem, seq_sem, seq_sem, seq_sem,
            pltpu.VMEM((n_seq // 2, chunk, wide), f32),
            pltpu.VMEM((columns * n_head, rows), f32),
            pltpu.VMEM((4, columns, rows), f32),
            pltpu.VMEM((columns, rows), f32),
            pltpu.VMEM((heads, n_seq * picked, rows), f32),
            pltpu.VMEM((heads, n_seq * picked, rows), f32),
            pltpu.VMEM((1, n_seq * 8, rows), f32),
            pltpu.VMEM((columns, rows), f32),
            pltpu.VMEM((wide, rows), f32),
            pltpu.VMEM((n_head, columns, rows), f32),
            pltpu.VMEM((columns, wide), f32),
            pltpu.VMEM((n_seq // 2, chunk, wide), f32),
            head_sem, head_sem, near_sem, near_sem, seq_sem, seq_sem, seq_sem, seq_sem,
            seq_sem, seq_sem, seq_sem, seq_sem, seq_sem, seq_sem, head_sem, head_sem,
        ],
        compiler_params=pltpu.CompilerParams(
            collective_id=0, has_side_effects=True, vmem_limit_bytes=60 * 1024 * 1024
        ),
    )(queries, keys, values, counts, out_weight, cotangent)
    return settle(results)


def solution(mesh):
    n_seq, n_head = mesh.shape["seq"], mesh.shape["head"]
    whole_is_middle = n_seq <= 1 << LOG2_CENTRAL and n_seq % 2 == 0
    body = functools.partial(fused, n_seq, n_head) if whole_is_middle else on_device
    in_specs = (
        P("head", "seq"),
        P("head", "seq"),
        P("head", "seq"),
        P("seq"),
        P("head", None),
        P("head", "seq"),
    )
    out_specs = (
        P("head", "seq"),
        P("head", "seq"),
        P("head", "seq"),
        P("head", "seq"),
        P("head", None),
    )
    return jax.shard_map(
        body, mesh=mesh, in_specs=in_specs, out_specs=out_specs, check_vma=False
    )
```
